256 devices in a mesh: grp: 32 (over z_lo, x, core), blk: 8 (over z_hi, y).
Axes of the slice: x: 4, y: 4, z: 8 (z_hi: 2, z_lo: 4; z = z_hi * 4 + z_lo), core: 2. Of those that a mesh axis runs over, the one named last changes fastest.
Arguments:
- features: float32 [65536, 128], P(('grp', 'blk')), may hold values from -6 to 6
- w_neigh: float32 [128, 128], replicated, may hold values from -2 to 2
- w_root: float32 [128, 128], replicated, may hold values from -0.5 to 0.5
- bias: float32 [128], replicated, may hold values from -3 to 3
- grad_out: float32 [65536, 128], P(('grp', 'blk')), may hold values from -6 to 6
- tile_coord: int32 [32, 8, 8, 2, 6], P('grp', 'blk'), may hold values from 0 to 1
- tile_edge: int32 [32, 8, 8, 6, 2, 128], P('grp', 'blk'), may hold values from 0 to 127
- send_idx: int32 [32, 8, 32, 32], P('grp', 'blk'), may hold values from 0 to 255
- halo_dst: int32 [32, 8, 1024], P('grp', 'blk'), may hold values from 0 to 255
- halo_src: int32 [32, 8, 1024], P('grp', 'blk'), may hold values from 0 to 1023, as said below
- hub_idx: int32 [32, 8, 8], P('grp', 'blk'), may hold values from 0 to 255
- hub_dst: int32 [32, 8, 256], P('grp', 'blk'), may hold values from 0 to 255
- hub_src: int32 [32, 8, 256], P('grp', 'blk'), may hold values from 0 to 2047
Outputs:
- output: float32 [65536, 128], P(('grp', 'blk'))
- grad_features: float32 [65536, 128], P(('grp', 'blk'))
- grad_w_neigh: float32 [128, 128], replicated
- grad_w_root: float32 [128, 128], replicated
- grad_bias: float32 [128], replicated
The draws below stay inside these ranges and needn't reach their ends.
Inputs may be any that keep to these rules, and one draw needn't show every extreme that they name: `halo_src`: A value q names slot q % 32 of the rows that partition q // 32 sends to this device's partition at the same blk index, never the device's own partition; from each source partition the named slots lie below a count of that pair, and every device names slot 31 of some source partition.
All inputs are finite; a program needn't handle non-finite values.
Results may differ from the reference program's by a relative error of at most 0.0003.
Values sent between devices are 32-bit elements; how exact they have to be, the bound alone decides.
No kernel may reach another device: no remote copies, remote signals or barrier semaphores. Data moves between devices by JAX's collectives and lax.ppermute only.
A program may use at most 64 MiB of HBM per device.

```python
import math
import jax
import jax.numpy as jnp
import numpy as np
from jax import lax

F = 128
H = 128
EPT = 128
NB_DEV = 256
TPB = 6
CAP = 32
HE = 1024
HUB_DEV = 8
HUBE = 256
HUBS = 2048
NODES = 65536
N_GRP = 32
N_BLK = 8


def draw_halo_src(key, part):
    key = jax.random.fold_in(key, 11)
    subkeys = jax.random.split(key, 5)
    grp_index = jnp.arange(N_GRP, dtype=jnp.int32)
    counts = jax.random.randint(subkeys[0], (N_GRP, N_BLK, N_GRP), 1, CAP + 1)
    rotation = jax.random.randint(subkeys[1], (N_GRP, N_BLK), 0, N_GRP - 1)
    fullest = (grp_index[:, None] + 1 + rotation) % N_GRP
    fullest = jnp.where(grp_index[:, None] == 0, N_GRP - 1, fullest)
    counts = jnp.where(grp_index[None, None, :] == fullest[:, :, None], CAP, counts)
    reaches = jax.random.randint(subkeys[2], (N_GRP, N_BLK, HE), 1, N_GRP)
    offsets = jax.random.randint(subkeys[3], (N_GRP, N_BLK, HE), 0, reaches)
    source = (grp_index[:, None, None] + 1 + offsets) % N_GRP
    source = source.at[:, :, 0].set(fullest)
    limits = jnp.take_along_axis(counts, source, axis=2)
    slot_ids = jax.random.randint(subkeys[4], (N_GRP, N_BLK, HE), 0, limits)
    slot_ids = slot_ids.at[:, :, 0].set(CAP - 1)
    return (source * CAP + slot_ids).astype(jnp.int32)


def plant(values, own_key, smallest, top_value):
    dims = values.shape
    index_at = [jax.random.randint(jax.random.fold_in(own_key, axis), (), 0, dims[axis]) for axis in range(len(dims))]
    values = values.at[tuple(index_at)].set(smallest)
    longest = dims.index(max(dims))
    index_at[longest] = (index_at[longest] + 1) % dims[longest]
    return values.at[tuple(index_at)].set(top_value)


def steps_of(key, extent, cuts, least, top_value):
    def one(position, blocks):
        heights = jax.random.uniform(jax.random.fold_in(jax.random.fold_in(key, 6), position), (blocks,), jnp.float32, least / len(cuts), top_value / len(cuts))
        return jnp.repeat(jnp.exp(heights), extent[position] // blocks).reshape((-1,) + (1,) * (len(extent) - position - 1))

    gain = one(*cuts[0])
    for cut in cuts[1:]:
        gain = gain * one(*cut)
    return gain


def rank_table(count, skew):
    loads = [(1 << 20) // math.isqrt(standing ** skew) + 1 for standing in range(1, count + 1)]
    width = 1 + sum(loads) // (1 << 30)
    return np.cumsum(np.array([max(1, weight // width) for weight in loads]))


def ranked(stream_key, dims, amount, slope):
    table = rank_table(amount, slope)
    lot = jax.random.randint(jax.random.fold_in(stream_key, 1), dims, 0, int(table[amount - 1]))
    standing = jnp.searchsorted(jnp.asarray(table, jnp.int32), lot, side="right")
    return jax.random.permutation(jax.random.fold_in(stream_key, 2), amount)[standing].astype(jnp.int32)


def noise(key, dims, spread, limit, cuts=(), kind=jnp.bfloat16):
    values = spread * jax.random.normal(key, dims, jnp.float32)
    if cuts:
        values = values * steps_of(key, dims, cuts, -0.22, 0.18)
    return jnp.clip(values, -limit, limit).astype(kind)


def setup_inputs(seed: int = 0) -> dict:
    seeds = jax.random.split(jax.random.key(seed), 14)
    features = noise(seeds[0], (NODES, F), 1.0, 6.0, ((0, 256),), jnp.float32)
    w_neigh = noise(seeds[1], (F, H), (F // 16) ** -0.5, 2.0, (), jnp.float32)
    w_root = noise(seeds[2], (F, H), F ** -0.5, 0.5, (), jnp.float32)
    bias = noise(seeds[3], (H,), 0.5, 3.0, (), jnp.float32)
    grad_out = noise(seeds[4], (NODES, H), 1.0, 6.0, ((0, 256),), jnp.float32)
    tile_coord = plant(jax.random.randint(seeds[5], (N_GRP, N_BLK, N_BLK, 2, TPB), 0, NB_DEV // 128), jax.random.fold_in(seeds[5], 1), 0, (NB_DEV // 128) - 1).astype(jnp.int32)
    tile_edge = plant(jax.random.randint(seeds[6], (N_GRP, N_BLK, N_BLK, TPB, 2, EPT), 0, 128), jax.random.fold_in(seeds[6], 1), 0, 127).astype(jnp.int32)
    send_idx = plant(jax.random.randint(seeds[7], (N_GRP, N_BLK, N_GRP, CAP), 0, NB_DEV), jax.random.fold_in(seeds[7], 1), 0, NB_DEV - 1).astype(jnp.int32)
    halo_dst = plant(jax.random.randint(seeds[8], (N_GRP, N_BLK, HE), 0, NB_DEV), jax.random.fold_in(seeds[8], 1), 0, NB_DEV - 1).astype(jnp.int32)
    halo_src = draw_halo_src(jax.random.fold_in(seeds[13], 71), 0)
    hub_idx = plant(jax.random.randint(seeds[10], (N_GRP, N_BLK, HUB_DEV), 0, NB_DEV), jax.random.fold_in(seeds[10], 1), 0, NB_DEV - 1).astype(jnp.int32)
    hub_dst = plant(jax.random.randint(seeds[11], (N_GRP, N_BLK, HUBE), 0, NB_DEV), jax.random.fold_in(seeds[11], 1), 0, NB_DEV - 1).astype(jnp.int32)
    hub_src = plant(ranked(seeds[12], (N_GRP, N_BLK, HUBE), HUBS, 2), jax.random.fold_in(seeds[12], 3), 0, HUBS - 1).astype(jnp.int32)
    return dict(features=features, w_neigh=w_neigh, w_root=w_root, bias=bias, grad_out=grad_out, tile_coord=tile_coord, tile_edge=tile_edge, send_idx=send_idx, halo_dst=halo_dst, halo_src=halo_src, hub_idx=hub_idx, hub_dst=hub_dst, hub_src=hub_src)


def edge_total(values, read_rows, write_rows, total_rows):
    def visit(running, indices):
        return running.at[indices[1]].add(jnp.take(values, indices[0], axis=0)), None

    start_value = jnp.zeros((total_rows, values.shape[1]), values.dtype)
    result, _ = lax.scan(visit, start_value, (read_rows, write_rows))
    return result


def reference(features, w_neigh, w_root, bias, grad_out, tile_coord, tile_edge, send_idx, halo_dst, halo_src, hub_idx, hub_dst, hub_src):
    device_count = N_GRP * N_BLK
    grp_ids = jnp.arange(N_GRP, dtype=jnp.int32)
    blk_ids = jnp.arange(N_BLK, dtype=jnp.int32)
    dest_base = (grp_ids[:, None] * N_BLK + blk_ids[None, :]) * NB_DEV
    intra_to = dest_base[:, :, None, None, None] + 128 * tile_coord[:, :, :, 0, :, None] + tile_edge[:, :, :, :, 0, :]
    source_base = (grp_ids[:, None, None] * N_BLK + blk_ids[None, None, :]) * NB_DEV
    intra_from = source_base[:, :, :, None, None] + 128 * tile_coord[:, :, :, 1, :, None] + tile_edge[:, :, :, :, 1, :]
    from_part = (halo_src // CAP).astype(jnp.int32)
    slot_ids = (halo_src % CAP).astype(jnp.int32)
    sender_rows = send_idx[from_part, blk_ids[None, :, None], grp_ids[:, None, None], slot_ids]
    halo_from = (from_part * N_BLK + blk_ids[None, :, None]) * NB_DEV + sender_rows
    halo_to = dest_base[:, :, None] + halo_dst
    hub_flat = hub_idx.reshape(-1)
    hub_global = (jnp.arange(HUBS, dtype=jnp.int32) // HUB_DEV) * NB_DEV + hub_flat
    hub_from = jnp.take(hub_global, hub_src, axis=0)
    hub_to = dest_base[:, :, None] + hub_dst
    edge_sets = [
        (intra_from.reshape(device_count, -1).astype(jnp.int32), intra_to.reshape(device_count, -1).astype(jnp.int32)),
        (halo_from.reshape(device_count, -1).astype(jnp.int32), halo_to.reshape(device_count, -1).astype(jnp.int32)),
        (hub_from.reshape(device_count, -1).astype(jnp.int32), hub_to.reshape(device_count, -1).astype(jnp.int32)),
    ]
    all_to = jnp.concatenate([pair_set[1].reshape(-1) for pair_set in edge_sets])
    degree = jnp.zeros((NODES,), jnp.float32).at[all_to].add(1.0)
    neighbour_sum = edge_total(features, edge_sets[0][0], edge_sets[0][1], NODES)
    neighbour_sum = neighbour_sum + edge_total(features, edge_sets[1][0], edge_sets[1][1], NODES)
    neighbour_sum = neighbour_sum + edge_total(features, edge_sets[2][0], edge_sets[2][1], NODES)
    divisor = degree + 1.0
    mean_feat = neighbour_sum / divisor[:, None]
    precise = lax.Precision.HIGHEST
    pre = jnp.dot(mean_feat, w_neigh, precision=precise) + jnp.dot(features, w_root, precision=precise) + bias
    negative = jnp.minimum(pre, 0.0)
    output = jnp.where(pre > 0, pre, jnp.expm1(negative))
    grad_pre = grad_out * jnp.where(pre > 0, 1.0, jnp.exp(negative))
    grad_sum = jnp.dot(grad_pre, w_neigh.T, precision=precise) / divisor[:, None]
    grad_features = jnp.dot(grad_pre, w_root.T, precision=precise)
    grad_features = grad_features + edge_total(grad_sum, edge_sets[0][1], edge_sets[0][0], NODES)
    grad_features = grad_features + edge_total(grad_sum, edge_sets[1][1], edge_sets[1][0], NODES)
    grad_features = grad_features + edge_total(grad_sum, edge_sets[2][1], edge_sets[2][0], NODES)
    factor = NODES ** -0.5
    grad_w_neigh = jnp.dot(mean_feat.T, grad_pre, precision=precise) * factor
    grad_w_root = jnp.dot(features.T, grad_pre, precision=precise) * factor
    grad_bias = jnp.sum(grad_pre, axis=0) * factor
    return output, grad_features, grad_w_neigh, grad_w_root, grad_bias
```

```python
import jax
import jax.numpy as jnp
from jax import lax
from jax.experimental import pallas as pl
from jax.experimental.pallas import tpu as pltpu
from jax.sharding import PartitionSpec as P

HIGH = lax.Precision.HIGHEST
F32, BF16, I32 = jnp.float32, jnp.bfloat16, jnp.int32
NT = (((1,), (1,)), ((), ()))
NN = (((1,), (0,)), ((), ()))
TN = (((0,), (0,)), ((), ()))


def dot(a, b, dims=NN, precision=None):
    return lax.dot_general(a, b, dims, precision=precision, preferred_element_type=F32)


def halves(x):
    high = x.astype(BF16)
    low = (x - high.astype(F32)).astype(BF16)
    return jnp.concatenate([high, low], axis=1)


def joined(y):
    n = y.shape[1] // 2
    return y[:, :n] + y[:, n:]


def one_hot(idx, rows):
    n = idx.shape[1]
    row = lax.broadcasted_iota(I32, (rows, n), 0)
    return jnp.where(row == idx, 1.0, 0.0).astype(BF16)


def lanes(ref_rows):
    return jnp.concatenate(ref_rows, axis=1)


def call(kernel, out_shape, args, specs=None, scratch=(), flops=1 << 28):
    whole = pl.BlockSpec(memory_space=pltpu.VMEM)
    size = sum(int(a.size) * a.dtype.itemsize for a in args)
    return pl.pallas_call(
        kernel,
        out_shape=out_shape,
        in_specs=[whole] * len(args) if specs is None else specs,
        out_specs=jax.tree.map(
            lambda s: pl.BlockSpec(memory_space=pltpu.SMEM if s.shape == (1,) else pltpu.VMEM), out_shape
        ),
        scratch_shapes=list(scratch),
        compiler_params=pltpu.CompilerParams(vmem_limit_bytes=40 << 20),
        cost_estimate=pl.CostEstimate(flops=flops, bytes_accessed=size, transcendentals=0),
    )(*args)


def shape(s, d=F32):
    return jax.ShapeDtypeStruct(s, d)


def expm1(x):
    series = x * (1 + x * (1 / 2) * (1 + x * (1 / 3) * (1 + x * (1 / 4) * (1 + x * (1 / 5) * (1 + x * (1 / 6) * (1 + x * (1 / 7)))))))
    return jnp.where(x > -0.35, series, jnp.exp(x) - 1.0)


def k_send(features, send, hub, out):
    x = halves(features[...])
    hot = lanes([one_hot(send[i : i + 1, :], 256) for i in range(8)])
    rows = joined(dot(hot, x, TN))
    out[:, 0:32, :] = rows.reshape(32, 32, 128)
    hub_rows = joined(dot(one_hot(hub[0:1, :], 256), x, TN))[0:8, :]
    for p in range(32):
        out[p, 32:40, :] = hub_rows


def k_index(pos, lists, own_to, halo_to, halo_from, hub_to,
            fwd, bwd, fwd_low, bwd_low, h_fwd, h_bwd, h_fwd_low, h_bwd_low, inv, flag):
    me = pos[0]
    zh, y = me // 4, me % 4
    top = jnp.float32(0.0)

    def keep(count, high_ref, low_ref, at):
        high = count.astype(BF16)
        high_ref[at] = high
        low_ref[at] = (count - high.astype(F32)).astype(BF16)

    for r in range(8):
        b = jnp.bitwise_xor(zh, r // 4) * 4 + (y + r % 4) % 4
        block = lists[b]
        to = lanes([one_hot(block[i : i + 1, :], 256) for i in range(6)])
        frm = lanes([one_hot(block[i : i + 1, :], 256) for i in range(6, 12)])
        h_to = lanes([one_hot(block[i : i + 1, :], 256) for i in range(12, 14)])
        codes = [block[i : i + 1, :] for i in range(14, 16)]
        rows = [jnp.where((c >> 3) % 8 == me, (c >> 6) * 8 + c % 8, -1) for c in codes]
        h_frm = lanes([one_hot(c, 256) for c in rows])
        count = jnp.concatenate([dot(to, frm, NT), dot(h_to, h_frm, NT)], axis=1)
        top = jnp.maximum(top, jnp.max(count))
        keep(count, fwd, fwd_low, r)
        count_t = jnp.concatenate([dot(frm, to, NT), dot(h_frm, h_to, NT)], axis=0)
        keep(count_t, bwd, bwd_low, r)
    to = lanes([one_hot(halo_to[i : i + 1, :], 256) for i in range(8)])
    frm = lanes([one_hot(halo_from[i : i + 1, :], 1024) for i in range(8)])
    count = dot(to, frm, NT)
    top = jnp.maximum(top, jnp.max(count))
    keep(count, h_fwd, h_fwd_low, ...)
    keep(dot(frm, to, NT), h_bwd, h_bwd_low, ...)
    flag[0] = (top > 256.0).astype(I32)
    row = lax.broadcasted_iota(I32, (256, 128), 0)
    degree = jnp.zeros((256, 128), F32)
    for ref, n in ((own_to, 48), (halo_to, 8), (hub_to, 2)):
        for i in range(n):
            degree = degree + jnp.where(row == ref[i : i + 1, :], 1.0, 0.0)
    degree = jnp.sum(degree, axis=1, keepdims=True)
    inv[...] = jnp.broadcast_to(1.0 / (degree + 1.0), (256, 128))


def k_partial(flag, features, incoming, fwd, fwd_low, *rest):
    outs, held = rest[:8], rest[8]
    hubs = incoming[:, 32:40, :].reshape(256, 128)
    x = jnp.concatenate([halves(features[...]), halves(hubs)], axis=0)
    for r in (5, 7, 6, 4, 1, 3, 2, 0):
        outs[r][...] = joined(dot(fwd[r], x))

    @pl.when(flag[0] != 0)
    def _():
        pltpu.sync_copy(fwd_low, held)
        for r in range(8):
            outs[r][...] += joined(dot(held[r], x))


def k_halo(flag, incoming, h_fwd, h_low, own, out, held):
    x = halves(incoming[:, 0:32, :].reshape(1024, 128))
    out[...] = own[...] + joined(dot(h_fwd[...], x))

    @pl.when(flag[0] != 0)
    def _():
        pltpu.sync_copy(h_low, held)
        out[...] += joined(dot(held[...], x))


def k_layer(a0, a1, a2, a3, a4, inv, features, w_neigh, w_root, bias, grad_out,
            output, grad_pre, grad_sum, mean):
    scale = inv[...]
    m = (a0[...] + a1[...] + a2[...] + a3[...] + a4[...]) * scale
    mean[...] = m
    pre = dot(m, w_neigh[...], NN, HIGH) + dot(features[...], w_root[...], NN, HIGH) + bias[...]
    negative = jnp.minimum(pre, 0.0)
    output[...] = jnp.where(pre > 0, pre, expm1(negative))
    g = grad_out[...] * jnp.where(pre > 0, 1.0, jnp.exp(negative))
    grad_pre[...] = g
    grad_sum[...] = dot(g, w_neigh[...], NT, HIGH) * scale


def k_weights(grad_pre, mean, features, out):
    g = grad_pre[...]
    wn = dot(mean[...], g, TN, HIGH)
    wr = dot(features[...], g, TN, HIGH)
    out[0:16, 0:8, :] = wn.reshape(16, 8, 128)
    out[16:32, 0:8, :] = wr.reshape(16, 8, 128)
    total = jnp.sum(g, axis=0, keepdims=True)
    fill = jnp.broadcast_to(total, (8, 128))
    for p in range(32):
        out[p, 8:16, :] = fill


def k_slots(flag, grad_sum, h_bwd, h_low, grad_pre, w_root, slots, root, held):
    x = halves(grad_sum[...])
    slots[...] = joined(dot(h_bwd[...], x))
    root[...] = dot(grad_pre[...], w_root[...], NT, HIGH)

    @pl.when(flag[0] != 0)
    def _():
        pltpu.sync_copy(h_low, held)
        slots[...] += joined(dot(held[...], x))


def k_back(flag, g0, g1, g2, g3, g4, g5, g6, g7, bwd, bwd_low, slots, root, out, local, held, total):
    xs = [halves(g[...]) for g in (g0, g1, g2, g3, g4, g5, g6, g7)]
    acc = dot(bwd[0], xs[0])
    for r in range(1, 8):
        acc = acc + dot(bwd[r], xs[r])
    total[...] = joined(acc)

    @pl.when(flag[0] != 0)
    def _():
        pltpu.sync_copy(bwd_low, held)
        for r in range(8):
            total[...] += joined(dot(held[r], xs[r]))

    out[:, 0:32, :] = slots[...].reshape(32, 32, 128)
    out[:, 32:40, :] = total[256:512, :].reshape(32, 8, 128)
    local[...] = root[...] + total[0:256, :]


def k_final(returned, send, hub, local, out):
    hot = lanes([one_hot(send[i : i + 1, :], 256) for i in range(8)])
    acc = dot(hot, halves(returned[:, 0:32, :].reshape(1024, 128)))
    hub_rows = jnp.sum(returned[:, 32:40, :], axis=0)
    hub_rows = jnp.concatenate([hub_rows, jnp.zeros((120, 128), F32)], axis=0)
    acc = acc + dot(one_hot(hub[0:1, :], 256), halves(hub_rows))
    out[...] = local[...] + joined(acc)


def per_device(features, w_neigh, w_root, bias, grad_out, tile_coord, tile_edge,
               send_idx, halo_dst, halo_src, hub_idx, hub_dst, hub_src):
    coords = tile_coord.reshape(8, 2, 6)
    edges = tile_edge.reshape(8, 6, 2, 128)
    own_to = coords[:, 0, :, None] * 128 + edges[:, :, 0, :]
    own_from = coords[:, 1, :, None] * 128 + edges[:, :, 1, :]
    hub_to = hub_dst.reshape(2, 128)
    hub_from = hub_src.reshape(2, 128)
    lists = jnp.concatenate(
        [own_to, own_from, jnp.broadcast_to(hub_to[None], (8, 2, 128)), jnp.broadcast_to(hub_from[None], (8, 2, 128))],
        axis=1,
    )
    send = send_idx.reshape(8, 128)
    hub = jnp.pad(hub_idx.reshape(1, 8), ((0, 0), (0, 120)), constant_values=-1)
    halo_to = halo_dst.reshape(8, 128)
    halo_from = halo_src.reshape(8, 128)
    pos = lax.axis_index("blk").astype(I32).reshape(1)

    def swap(v):
        return lax.ppermute(v, "blk", [(i, i ^ 4) for i in range(8)])

    def turn(v, k):
        return lax.ppermute(v, "blk", [(i, i // 4 * 4 + (i % 4 + k) % 4) for i in range(8)])

    def exchange(v, axis):
        return lax.all_to_all(v, axis, split_axis=0, concat_axis=0, tiled=True)

    vm, sm, hb = (pl.BlockSpec(memory_space=s) for s in (pltpu.VMEM, pltpu.SMEM, pl.ANY))

    outgoing = call(k_send, shape((32, 40, 128)), (features, send, hub))
    incoming = exchange(outgoing, "grp")
    lists = exchange(lists, "blk")
    fwd, bwd, fwd_low, bwd_low, h_fwd, h_bwd, h_fwd_low, h_bwd_low, inv, flag = call(
        k_index,
        (shape((8, 256, 512), BF16), shape((8, 512, 256), BF16), shape((8, 256, 512), BF16), shape((8, 512, 256), BF16),
         shape((256, 1024), BF16), shape((1024, 256), BF16), shape((256, 1024), BF16), shape((1024, 256), BF16),
         shape((256, 128)), shape((1,), I32)),
        (pos, lists, own_to.reshape(48, 128), halo_to, halo_from, hub_to),
        [sm, vm, vm, vm, vm, vm],
        flops=1 << 31,
    )
    part = call(
        k_partial, [shape((256, 128))] * 8, (flag, features, incoming, fwd, fwd_low), [sm, vm, vm, vm, hb],
        [pltpu.VMEM((8, 256, 512), BF16)], flops=1 << 29,
    )
    far = part[4] + turn(part[5], 1) + turn(part[7], 3) + turn(part[6], 2)
    far = swap(far)
    near = [turn(part[1], 1), turn(part[3], 3), turn(part[2], 2)]
    own = call(
        k_halo, shape((256, 128)), (flag, incoming, h_fwd, h_fwd_low, part[0]), [sm, vm, vm, hb, vm],
        [pltpu.VMEM((256, 1024), BF16)],
    )
    output, grad_pre, grad_sum, mean = call(
        k_layer, [shape((256, 128))] * 4,
        (own, *near, far, inv, features, w_neigh, w_root, bias.reshape(1, 128), grad_out),
    )
    other = swap(grad_sum)
    g1, g3, g2 = turn(grad_sum, 3), turn(grad_sum, 1), turn(grad_sum, 2)
    g5, g7, g6 = turn(other, 3), turn(other, 1), turn(other, 2)
    weights = call(k_weights, shape((32, 16, 128)), (grad_pre, mean, features))
    weights = exchange(weights, "grp").sum(axis=0)
    weights = exchange(jnp.broadcast_to(weights[None], (8, 16, 128)), "blk").sum(axis=0)
    slots, root = call(
        k_slots, [shape((1024, 128)), shape((256, 128))], (flag, grad_sum, h_bwd, h_bwd_low, grad_pre, w_root),
        [sm, vm, vm, hb, vm, vm], [pltpu.VMEM((1024, 256), BF16)],
    )
    back, local = call(
        k_back, [shape((32, 40, 128)), shape((256, 128))],
        (flag, grad_sum, g1, g2, g3, other, g5, g6, g7, bwd, bwd_low, slots, root),
        [sm] + [vm] * 8 + [vm, hb, vm, vm],
        [pltpu.VMEM((8, 512, 256), BF16), pltpu.VMEM((512, 128), F32)],
    )
    returned = exchange(back, "grp")
    grad_features = call(k_final, shape((256, 128)), (returned, send, hub, local))
    factor = (256 * lax.axis_size("grp") * lax.axis_size("blk")) ** (-0.5)
    full = exchange(jnp.broadcast_to(weights[None, 0:8], (32, 8, 128)), "grp") * factor
    full = full.reshape(256, 128)
    return output, grad_features, full[0:128], full[128:256], weights[8] * factor


def solution(mesh):
    rows = P(("grp", "blk"), None)
    in_specs = (
        rows, P(), P(), P(), rows,
        P("grp", "blk", None, None, None),
        P("grp", "blk", None, None, None, None),
        P("grp", "blk", None, None),
        P("grp", "blk", None), P("grp", "blk", None), P("grp", "blk", None), P("grp", "blk", None), P("grp", "blk", None),
    )
    return jax.shard_map(
        per_device, mesh=mesh, in_specs=in_specs, out_specs=(rows, rows, P(), P(), P()), check_vma=False
    )
```

```python
import functools

import jax
import jax.numpy as jnp
from jax import lax
from jax.experimental import pallas as pl
from jax.experimental.pallas import tpu as pltpu
from jax.sharding import PartitionSpec as P

HIGH = lax.Precision.HIGHEST
F32, BF16, I32 = jnp.float32, jnp.bfloat16, jnp.int32
NT = (((1,), (1,)), ((), ()))
NN = (((1,), (0,)), ((), ()))
TN = (((0,), (0,)), ((), ()))


def dot(a, b, dims=NN, precision=None):
    return lax.dot_general(a, b, dims, precision=precision, preferred_element_type=F32)


def halves(x):
    high = x.astype(BF16)
    low = (x - high.astype(F32)).astype(BF16)
    return jnp.concatenate([high, low], axis=1)


def joined(y):
    n = y.shape[1] // 2
    return y[:, :n] + y[:, n:]


def one_hot(idx, rows):
    n = idx.shape[1]
    row = lax.broadcasted_iota(I32, (rows, n), 0)
    return jnp.where(row == idx, 1.0, 0.0).astype(BF16)


def lanes(ref_rows):
    return jnp.concatenate(ref_rows, axis=1)


def call(kernel, out_shape, args, specs=None, scratch=(), flops=1 << 28):
    whole = pl.BlockSpec(memory_space=pltpu.VMEM)
    size = sum(int(a.size) * a.dtype.itemsize for a in args)
    return pl.pallas_call(
        kernel,
        out_shape=out_shape,
        in_specs=[whole] * len(args) if specs is None else specs,
        out_specs=jax.tree.map(
            lambda s: pl.BlockSpec(memory_space=pltpu.SMEM if s.shape == (1,) else pltpu.VMEM), out_shape
        ),
        scratch_shapes=list(scratch),
        compiler_params=pltpu.CompilerParams(vmem_limit_bytes=16 << 20),
        cost_estimate=pl.CostEstimate(flops=flops, bytes_accessed=size, transcendentals=0),
    )(*args)


def shape(s, d=F32):
    return jax.ShapeDtypeStruct(s, d)


def expm1(x):
    series = x * (1 + x * (1 / 2) * (1 + x * (1 / 3) * (1 + x * (1 / 4) * (1 + x * (1 / 5) * (1 + x * (1 / 6) * (1 + x * (1 / 7)))))))
    return jnp.where(x > -0.35, series, jnp.exp(x) - 1.0)


def k_send(features, send, hub, out):
    x = halves(features[...])
    hot = lanes([one_hot(send[i : i + 1, :], 256) for i in range(8)])
    rows = joined(dot(hot, x, TN))
    out[:, 0:32, :] = rows.reshape(32, 32, 128)
    hub_rows = jnp.concatenate([features[pl.ds(hub[j], 1), :] for j in range(8)], axis=0)
    for p in range(32):
        out[p, 32:40, :] = hub_rows


def k_lists(pos, coord, edge, hub_to, hub_from, own_to, *outs):
    me = pos[0]
    for b in range(8):
        for t in range(6):
            own_to[b * 6 + t : b * 6 + t + 1, :] = edge[b, t, 0:1, :] + coord[b, 0, t] * 128
    for d in range(2):
        for k in range(4):
            b = jnp.bitwise_xor(me // 4, d) * 4 + (me % 4 + k) % 4
            at = d * 16
            for t in range(6):
                outs[k][at + t : at + t + 1, :] = edge[b, t, 0:1, :] + coord[b, 0, t] * 128
                outs[k][at + 6 + t : at + 7 + t, :] = edge[b, t, 1:2, :] + coord[b, 1, t] * 128
            outs[k][at + 12 : at + 14, :] = hub_to[...]
            outs[k][at + 14 : at + 16, :] = hub_from[...]


def hots(pos, block):
    me = pos[0]
    to = lanes([one_hot(block[i : i + 1, :], 256) for i in range(6)])
    frm = lanes([one_hot(block[i : i + 1, :], 256) for i in range(6, 12)])
    h_to = lanes([one_hot(block[i : i + 1, :], 256) for i in range(12, 14)])
    codes = [block[i : i + 1, :] for i in range(14, 16)]
    rows = [jnp.where((c >> 3) % 8 == me, (c >> 6) * 8 + c % 8, -1) for c in codes]
    return to, frm, h_to, lanes([one_hot(c, 256) for c in rows])


def blocks_of(lists):
    own, l1, l2, l3, far = lists
    return [ref[0:16, :] for ref in (own, l1, l2, l3)] + [far[16 * k : 16 * k + 16, :] for k in range(4)]


def halo_hots(halo_to, halo_from):
    to = lanes([one_hot(halo_to[i : i + 1, :], 256) for i in range(8)])
    return to, lanes([one_hot(halo_from[i : i + 1, :], 1024) for i in range(8)])


def rest(count):
    return (count - count.astype(BF16).astype(F32)).astype(BF16)


def forward_count(to, frm, h_to, h_frm):
    return jnp.concatenate([dot(to, frm, NT), dot(h_to, h_frm, NT)], axis=1)


def backward_count(to, frm, h_to, h_frm):
    return jnp.concatenate([dot(frm, to, NT), dot(h_frm, h_to, NT)], axis=0)


def k_fwd(pos, l0, l1, l2, l3, far, fwd, flag):
    top = jnp.float32(0.0)
    for r, block in enumerate(blocks_of((l0, l1, l2, l3, far))):
        count = forward_count(*hots(pos, block))
        top = jnp.maximum(top, jnp.max(count))
        fwd[r] = count.astype(BF16)
    flag[0] = (top > 256.0).astype(I32)


def k_bwd(pos, l0, l1, l2, l3, far, bwd):
    for r, block in enumerate(blocks_of((l0, l1, l2, l3, far))):
        bwd[r] = backward_count(*hots(pos, block)).astype(BF16)


def k_boundary(own_to, halo_to, halo_from, hub_to, h_fwd, h_bwd, inv, flag):
    to, frm = halo_hots(halo_to, halo_from)
    count = dot(to, frm, NT)
    h_fwd[...] = count.astype(BF16)
    h_bwd[...] = dot(frm, to, NT).astype(BF16)
    flag[0] = (jnp.max(count) > 256.0).astype(I32)
    row = lax.broadcasted_iota(I32, (256, 128), 0)
    degree = jnp.zeros((256, 128), F32)
    for ref, n in ((own_to, 48), (halo_to, 8), (hub_to, 2)):
        for i in range(n):
            degree = degree + jnp.where(row == ref[i : i + 1, :], 1.0, 0.0)
    degree = jnp.sum(degree, axis=1, keepdims=True)
    inv[...] = jnp.broadcast_to(1.0 / (degree + 1.0), (256, 128))


def k_partial(flag, pos, l0, l1, l2, l3, far, features, incoming, fwd, *outs):
    hubs = incoming[:, 32:40, :].reshape(256, 128)
    x = jnp.concatenate([halves(features[...]), halves(hubs)], axis=0)
    for r in range(8):
        outs[r][...] = joined(dot(fwd[r], x))

    @pl.when(flag[0] != 0)
    def _():
        for r, block in enumerate(blocks_of((l0, l1, l2, l3, far))):
            outs[r][...] += joined(dot(rest(forward_count(*hots(pos, block))), x))


def k_halo(flag, halo_to, halo_from, incoming, h_fwd, own, out):
    x = halves(incoming[:, 0:32, :].reshape(1024, 128))
    out[...] = own[...] + joined(dot(h_fwd[...], x))

    @pl.when(flag[0] != 0)
    def _():
        to, frm = halo_hots(halo_to, halo_from)
        out[...] += joined(dot(rest(dot(to, frm, NT)), x))


def k_layer(a0, a1, a2, a3, a4, inv, features, w_neigh, w_root, bias, grad_out,
            output, grad_pre, grad_sum, mean):
    scale = inv[...]
    m = (a0[...] + a1[...] + a2[...] + a3[...] + a4[...]) * scale
    mean[...] = m
    pre = dot(m, w_neigh[...], NN, HIGH) + dot(features[...], w_root[...], NN, HIGH) + bias[...]
    negative = jnp.minimum(pre, 0.0)
    output[...] = jnp.where(pre > 0, pre, expm1(negative))
    g = grad_out[...] * jnp.where(pre > 0, 1.0, jnp.exp(negative))
    grad_pre[...] = g
    grad_sum[...] = dot(g, w_neigh[...], NT, HIGH) * scale


def k_mid(flag, halo_to, halo_from, grad_sum, h_bwd, grad_pre, mean, features, out, held):
    x = halves(grad_sum[...])
    held[...] = joined(dot(h_bwd[...], x))

    @pl.when(flag[0] != 0)
    def _():
        to, frm = halo_hots(halo_to, halo_from)
        held[...] += joined(dot(rest(dot(frm, to, NT)), x))

    out[:, 0:32, :] = held[...].reshape(32, 32, 128)
    g = grad_pre[...]
    out[0:16, 32:40, :] = dot(mean[...], g, TN, HIGH).reshape(16, 8, 128)
    out[16:32, 32:40, :] = dot(features[...], g, TN, HIGH).reshape(16, 8, 128)
    fill = jnp.broadcast_to(jnp.sum(g, axis=0, keepdims=True), (8, 128))
    for p in range(32):
        out[p, 40:48, :] = fill


def k_back(flag, pos, l0, l1, l2, l3, far, g0, g1, g2, g3, g4, g5, g6, g7, bwd, intra, hubs, total):
    xs = [halves(g[...]) for g in (g0, g1, g2, g3, g4, g5, g6, g7)]
    acc = dot(bwd[0], xs[0])
    for r in range(1, 8):
        acc = acc + dot(bwd[r], xs[r])
    total[...] = joined(acc)

    @pl.when(flag[0] != 0)
    def _():
        for r, block in enumerate(blocks_of((l0, l1, l2, l3, far))):
            total[...] += joined(dot(rest(backward_count(*hots(pos, block))), xs[r]))

    hubs[...] = total[256:512, :].reshape(32, 8, 128)
    intra[...] = total[0:256, :]


def k_sum(returned, out):
    out[...] = jnp.sum(returned[:, 32:48, :], axis=0)


def k_pack(factor, hubs, near, far, out, bias):
    w = (near[...] + far[...]) * factor
    out[:, 0:8, :] = hubs[...]
    for p in range(32):
        out[p, 8:16, :] = w[0:8]
    bias[...] = w[8:9]


def k_slots(returned, send, intra, grad_pre, w_root, out):
    hot = lanes([one_hot(send[i : i + 1, :], 256) for i in range(8)])
    acc = joined(dot(hot, halves(returned[:, 0:32, :].reshape(1024, 128))))
    out[...] = intra[...] + dot(grad_pre[...], w_root[...], NT, HIGH) + acc


def k_final(final, hub, local, out, w_neigh, w_root):
    rows = jnp.sum(final[:, 0:8, :], axis=0)
    out[...] = local[...]
    for j in range(8):
        out[pl.ds(hub[j], 1), :] += rows[j : j + 1, :]
    w_neigh[...] = final[0:16, 8:16, :].reshape(128, 128)
    w_root[...] = final[16:32, 8:16, :].reshape(128, 128)


def per_device(features, w_neigh, w_root, bias, grad_out, tile_coord, tile_edge,
               send_idx, halo_dst, halo_src, hub_idx, hub_dst, hub_src):
    send = send_idx.reshape(8, 128)
    hub = hub_idx.reshape(8)
    hub_to = hub_dst.reshape(2, 128)
    hub_from = hub_src.reshape(2, 128)
    halo_to = halo_dst.reshape(8, 128)
    halo_from = halo_src.reshape(8, 128)
    pos = lax.axis_index("blk").astype(I32).reshape(1)
    block = shape((256, 128))

    def swap(v):
        return lax.ppermute(v, "blk", [(i, i ^ 4) for i in range(8)])

    def turn(v, k):
        return lax.ppermute(v, "blk", [(i, i // 4 * 4 + (i % 4 + k) % 4) for i in range(8)])

    def exchange(v, axis):
        return lax.all_to_all(v, axis, split_axis=0, concat_axis=0, tiled=True)

    vm, sm = (pl.BlockSpec(memory_space=s) for s in (pltpu.VMEM, pltpu.SMEM))

    outgoing = call(k_send, shape((32, 40, 128)), (features, send, hub), [vm, vm, sm])
    outgoing, coord = lax.optimization_barrier((outgoing, tile_coord.reshape(8, 2, 6)))
    incoming = exchange(outgoing, "grp")
    own_to, m0, m1, m2, m3 = call(
        k_lists, [shape((48, 128), I32)] + [shape((32, 128), I32)] * 4,
        (pos, coord, tile_edge.reshape(8, 6, 2, 128), hub_to, hub_from), [sm, sm, vm, vm, vm],
    )
    l3, l2, l1 = turn(m1, 1), turn(m2, 2), turn(m3, 3)
    far = swap(jnp.concatenate([m0[16:], l1[16:], l2[16:], l3[16:]], axis=0))
    lists = (pos, m0, l1, l2, l3, far)
    lm = [sm] + [vm] * 5
    h_fwd, h_bwd, inv, h_flag = call(
        k_boundary, (shape((256, 1024), BF16), shape((1024, 256), BF16), block, shape((1,), I32)),
        (own_to, halo_to, halo_from, hub_to), flops=1 << 31,
    )
    fwd, flag = call(k_fwd, (shape((8, 256, 512), BF16), shape((1,), I32)), lists, lm, flops=1 << 31)
    bwd = call(k_bwd, shape((8, 512, 256), BF16), lists, lm, flops=1 << 31)
    part = call(k_partial, [block] * 8, (flag, *lists, features, incoming, fwd), [sm, *lm, vm, vm, vm])
    other = part[4] + turn(part[5], 1) + turn(part[7], 3) + turn(part[6], 2)
    other = swap(other)
    near = [turn(part[1], 1), turn(part[3], 3), turn(part[2], 2)]
    own = call(k_halo, block, (h_flag, halo_to, halo_from, incoming, h_fwd, part[0]), [sm] + [vm] * 5)
    output, grad_pre, grad_sum, mean = call(
        k_layer, [block] * 4, (own, *near, other, inv, features, w_neigh, w_root, bias.reshape(1, 128), grad_out),
    )
    g4 = swap(grad_sum)
    g1, g3, g2 = turn(grad_sum, 3), turn(grad_sum, 1), turn(grad_sum, 2)
    mid = call(
        k_mid, shape((32, 48, 128)), (h_flag, halo_to, halo_from, grad_sum, h_bwd, grad_pre, mean, features),
        [sm] + [vm] * 7, [pltpu.VMEM((1024, 128), F32)],
    )
    returned = exchange(mid, "grp")
    g5, g7, g6 = turn(g4, 3), turn(g4, 1), turn(g4, 2)
    intra, hubs = call(
        k_back, [block, shape((32, 8, 128))],
        (flag, *lists, grad_sum, g1, g2, g3, g4, g5, g6, g7, bwd), [sm, *lm] + [vm] * 9,
        [pltpu.VMEM((512, 128), F32)],
    )
    returned, intra = lax.optimization_barrier((returned, intra))
    w = call(k_sum, shape((16, 128)), (returned,))
    w = w + turn(w, 1) + turn(w, 2) + turn(w, 3)
    factor = (256 * lax.axis_size("grp") * lax.axis_size("blk")) ** (-0.5)
    last, grad_bias = call(
        functools.partial(k_pack, factor), [shape((32, 16, 128)), shape((1, 128))], (hubs, w, swap(w))
    )
    last = exchange(last, "grp")
    local = call(k_slots, block, (returned, send, intra, grad_pre, w_root))
    grad_features, grad_wn, grad_wr = call(
        k_final, [block, shape((128, 128)), shape((128, 128))], (last, hub, local), [vm, sm, vm]
    )
    return output, grad_features, grad_wn, grad_wr, grad_bias.reshape(128)


def solution(mesh):
    rows = P(("grp", "blk"), None)
    in_specs = (
        rows, P(), P(), P(), rows,
        P("grp", "blk", None, None, None),
        P("grp", "blk", None, None, None, None),
        P("grp", "blk", None, None),
        P("grp", "blk", None), P("grp", "blk", None), P("grp", "blk", None), P("grp", "blk", None), P("grp", "blk", None),
    )
    return jax.shard_map(
        per_device, mesh=mesh, in_specs=in_specs, out_specs=(rows, rows, P(), P(), P()), check_vma=False
    )
```

```python
import functools

import jax
import jax.numpy as jnp
from jax import lax
from jax.experimental import pallas as pl
from jax.experimental.pallas import tpu as pltpu
from jax.sharding import PartitionSpec as P

HIGH = lax.Precision.HIGHEST
F32, BF16, I32 = jnp.float32, jnp.bfloat16, jnp.int32
NT = (((1,), (1,)), ((), ()))
NN = (((1,), (0,)), ((), ()))
TN = (((0,), (0,)), ((), ()))


def dot(a, b, dims=NN, precision=None):
    return lax.dot_general(a, b, dims, precision=precision, preferred_element_type=F32)


def halves(x):
    high = x.astype(BF16)
    low = (x - high.astype(F32)).astype(BF16)
    return jnp.concatenate([high, low], axis=1)


def joined(y):
    n = y.shape[1] // 2
    return y[:, :n] + y[:, n:]


def one_hot(idx, rows):
    n = idx.shape[1]
    row = lax.broadcasted_iota(I32, (rows, n), 0)
    return jnp.where(row == idx, 1.0, 0.0).astype(BF16)


def lanes(ref_rows):
    return jnp.concatenate(ref_rows, axis=1)


def call(kernel, out_shape, args, specs=None, scratch=(), flops=1 << 28):
    whole = pl.BlockSpec(memory_space=pltpu.VMEM)
    size = sum(int(a.size) * a.dtype.itemsize for a in args)
    return pl.pallas_call(
        kernel,
        out_shape=out_shape,
        in_specs=[whole] * len(args) if specs is None else specs,
        out_specs=jax.tree.map(
            lambda s: pl.BlockSpec(memory_space=pltpu.SMEM if s.shape == (1,) else pltpu.VMEM), out_shape
        ),
        scratch_shapes=list(scratch),
        compiler_params=pltpu.CompilerParams(vmem_limit_bytes=16 << 20),
        cost_estimate=pl.CostEstimate(flops=flops, bytes_accessed=size, transcendentals=0),
    )(*args)


def shape(s, d=F32):
    return jax.ShapeDtypeStruct(s, d)


def expm1(x):
    series = x * (1 + x * (1 / 2) * (1 + x * (1 / 3) * (1 + x * (1 / 4) * (1 + x * (1 / 5) * (1 + x * (1 / 6) * (1 + x * (1 / 7)))))))
    return jnp.where(x > -0.35, series, jnp.exp(x) - 1.0)


def k_send(features, send, hub, out):
    x = halves(features[...])
    hot = lanes([one_hot(send[i : i + 1, :], 256) for i in range(8)])
    rows = joined(dot(hot, x, TN))
    out[:, 0:32, :] = rows.reshape(32, 32, 128)
    hub_rows = jnp.concatenate([features[pl.ds(hub[j], 1), :] for j in range(8)], axis=0)
    for p in range(32):
        out[p, 32:40, :] = hub_rows


def k_lists(pos, coord, edge, hub_to, hub_from, own_to, *outs):
    me = pos[0]
    for b in range(8):
        for t in range(6):
            own_to[b * 6 + t : b * 6 + t + 1, :] = edge[b, t, 0:1, :] + coord[b, 0, t] * 128
    for d in range(2):
        for k in range(4):
            b = jnp.bitwise_xor(me // 4, d) * 4 + (me % 4 + k) % 4
            at = d * 16
            for t in range(6):
                outs[k][at + t : at + t + 1, :] = edge[b, t, 0:1, :] + coord[b, 0, t] * 128
                outs[k][at + 6 + t : at + 7 + t, :] = edge[b, t, 1:2, :] + coord[b, 1, t] * 128
            outs[k][at + 12 : at + 14, :] = hub_to[...]
            outs[k][at + 14 : at + 16, :] = hub_from[...]


def hots(pos, block):
    me = pos[0]
    to = lanes([one_hot(block[i : i + 1, :], 256) for i in range(6)])
    frm = lanes([one_hot(block[i : i + 1, :], 256) for i in range(6, 12)])
    h_to = lanes([one_hot(block[i : i + 1, :], 256) for i in range(12, 14)])
    codes = [block[i : i + 1, :] for i in range(14, 16)]
    rows = [jnp.where((c >> 3) % 8 == me, (c >> 6) * 8 + c % 8, -1) for c in codes]
    return to, frm, h_to, lanes([one_hot(c, 256) for c in rows])


def blocks_of(lists):
    own, l1, l2, l3, far = lists
    return [ref[0:16, :] for ref in (own, l1, l2, l3)] + [far[16 * k : 16 * k + 16, :] for k in range(4)]


def halo_hots(halo_to, halo_from):
    to = lanes([one_hot(halo_to[i : i + 1, :], 256) for i in range(8)])
    return to, lanes([one_hot(halo_from[i : i + 1, :], 1024) for i in range(8)])


def rest(count):
    return (count - count.astype(BF16).astype(F32)).astype(BF16)


def forward_count(to, frm, h_to, h_frm):
    return jnp.concatenate([dot(to, frm, NT), dot(h_to, h_frm, NT)], axis=1)


def backward_count(to, frm, h_to, h_frm):
    return jnp.concatenate([dot(frm, to, NT), dot(h_frm, h_to, NT)], axis=0)


def k_fwd(pos, l0, l1, l2, l3, far, fwd, flag):
    top = jnp.float32(0.0)
    for r, block in enumerate(blocks_of((l0, l1, l2, l3, far))):
        count = forward_count(*hots(pos, block))
        top = jnp.maximum(top, jnp.max(count))
        fwd[r] = count.astype(BF16)
    flag[0] = (top > 256.0).astype(I32)


def k_bwd(pos, l0, l1, l2, l3, far, bwd):
    for r, block in enumerate(blocks_of((l0, l1, l2, l3, far))):
        bwd[r] = backward_count(*hots(pos, block)).astype(BF16)


def k_boundary(own_to, halo_to, halo_from, hub_to, h_fwd, h_bwd, inv, flag):
    to, frm = halo_hots(halo_to, halo_from)
    count = dot(to, frm, NT)
    h_fwd[...] = count.astype(BF16)
    h_bwd[...] = dot(frm, to, NT).astype(BF16)
    flag[0] = (jnp.max(count) > 256.0).astype(I32)
    row = lax.broadcasted_iota(I32, (256, 128), 0)
    degree = jnp.zeros((256, 128), F32)
    for ref, n in ((own_to, 48), (halo_to, 8), (hub_to, 2)):
        for i in range(n):
            degree = degree + jnp.where(row == ref[i : i + 1, :], 1.0, 0.0)
    degree = jnp.sum(degree, axis=1, keepdims=True)
    inv[...] = jnp.broadcast_to(1.0 / (degree + 1.0), (256, 128))


def k_partial(flag, pos, l0, l1, l2, l3, far, features, incoming, fwd, *outs):
    hubs = incoming[:, 32:40, :].reshape(256, 128)
    x = jnp.concatenate([halves(features[...]), halves(hubs)], axis=0)
    for r in range(8):
        outs[r][...] = joined(dot(fwd[r], x))

    @pl.when(flag[0] != 0)
    def _():
        for r, block in enumerate(blocks_of((l0, l1, l2, l3, far))):
            outs[r][...] += joined(dot(rest(forward_count(*hots(pos, block))), x))


def k_halo(flag, halo_to, halo_from, incoming, h_fwd, own, out):
    x = halves(incoming[:, 0:32, :].reshape(1024, 128))
    out[...] = own[...] + joined(dot(h_fwd[...], x))

    @pl.when(flag[0] != 0)
    def _():
        to, frm = halo_hots(halo_to, halo_from)
        out[...] += joined(dot(rest(dot(to, frm, NT)), x))


def k_layer(a0, a1, a2, a3, a4, inv, features, w_neigh, w_root, bias, grad_out,
            output, grad_pre, grad_sum, mean):
    scale = inv[...]
    m = (a0[...] + a1[...] + a2[...] + a3[...] + a4[...]) * scale
    mean[...] = m
    pre = dot(m, w_neigh[...], NN, HIGH) + dot(features[...], w_root[...], NN, HIGH) + bias[...]
    negative = jnp.minimum(pre, 0.0)
    output[...] = jnp.where(pre > 0, pre, expm1(negative))
    g = grad_out[...] * jnp.where(pre > 0, 1.0, jnp.exp(negative))
    grad_pre[...] = g
    grad_sum[...] = dot(g, w_neigh[...], NT, HIGH) * scale


def k_weights(grad_pre, mean, features, out):
    g = grad_pre[...]
    out[0:16, 0:8, :] = dot(mean[...], g, TN, HIGH).reshape(16, 8, 128)
    out[16:32, 0:8, :] = dot(features[...], g, TN, HIGH).reshape(16, 8, 128)
    fill = jnp.broadcast_to(jnp.sum(g, axis=0, keepdims=True), (8, 128))
    for p in range(32):
        out[p, 8:16, :] = fill


def k_slots(flag, halo_to, halo_from, grad_sum, h_bwd, grad_pre, w_root, out, root):
    x = halves(grad_sum[...])
    out[...] = joined(dot(h_bwd[...], x))
    root[...] = dot(grad_pre[...], w_root[...], NT, HIGH)

    @pl.when(flag[0] != 0)
    def _():
        to, frm = halo_hots(halo_to, halo_from)
        out[...] += joined(dot(rest(dot(frm, to, NT)), x))


def k_back(flag, pos, l0, l1, l2, l3, far, g0, g1, g2, g3, g4, g5, g6, g7, bwd, root, local, hubs, total):
    xs = [halves(g[...]) for g in (g0, g1, g2, g3, g4, g5, g6, g7)]
    acc = dot(bwd[0], xs[0])
    for r in range(1, 8):
        acc = acc + dot(bwd[r], xs[r])
    total[...] = joined(acc)

    @pl.when(flag[0] != 0)
    def _():
        for r, block in enumerate(blocks_of((l0, l1, l2, l3, far))):
            total[...] += joined(dot(rest(backward_count(*hots(pos, block))), xs[r]))

    hubs[...] = total[256:512, :].reshape(32, 8, 128)
    local[...] = root[...] + total[0:256, :]


def k_sum(weights, out):
    out[...] = jnp.sum(weights[...], axis=0)


def k_pack(factor, slots, hubs, near, far, out, bias):
    w = (near[...] + far[...]) * factor
    out[:, 0:32, :] = slots[...].reshape(32, 32, 128)
    out[:, 32:40, :] = hubs[...]
    for p in range(32):
        out[p, 40:48, :] = w[0:8]
    bias[...] = w[8:9]


def k_final(returned, send, hub, local, out, w_neigh, w_root):
    hot = lanes([one_hot(send[i : i + 1, :], 256) for i in range(8)])
    acc = joined(dot(hot, halves(returned[:, 0:32, :].reshape(1024, 128))))
    rows = jnp.sum(returned[:, 32:40, :], axis=0)
    out[...] = local[...] + acc
    for j in range(8):
        out[pl.ds(hub[j], 1), :] += rows[j : j + 1, :]
    w_neigh[...] = returned[0:16, 40:48, :].reshape(128, 128)
    w_root[...] = returned[16:32, 40:48, :].reshape(128, 128)


def per_device(features, w_neigh, w_root, bias, grad_out, tile_coord, tile_edge,
               send_idx, halo_dst, halo_src, hub_idx, hub_dst, hub_src):
    send = send_idx.reshape(8, 128)
    hub = hub_idx.reshape(8)
    hub_to = hub_dst.reshape(2, 128)
    hub_from = hub_src.reshape(2, 128)
    halo_to = halo_dst.reshape(8, 128)
    halo_from = halo_src.reshape(8, 128)
    pos = lax.axis_index("blk").astype(I32).reshape(1)
    block = shape((256, 128))

    def swap(v):
        return lax.ppermute(v, "blk", [(i, i ^ 4) for i in range(8)])

    def turn(v, k):
        return lax.ppermute(v, "blk", [(i, i // 4 * 4 + (i % 4 + k) % 4) for i in range(8)])

    def exchange(v, axis):
        return lax.all_to_all(v, axis, split_axis=0, concat_axis=0, tiled=True)

    vm, sm = (pl.BlockSpec(memory_space=s) for s in (pltpu.VMEM, pltpu.SMEM))

    outgoing = call(k_send, shape((32, 40, 128)), (features, send, hub), [vm, vm, sm])
    outgoing, coord = lax.optimization_barrier((outgoing, tile_coord.reshape(8, 2, 6)))
    incoming = exchange(outgoing, "grp")
    own_to, m0, m1, m2, m3 = call(
        k_lists, [shape((48, 128), I32)] + [shape((32, 128), I32)] * 4,
        (pos, coord, tile_edge.reshape(8, 6, 2, 128), hub_to, hub_from), [sm, sm, vm, vm, vm],
    )
    l3, l2, l1 = turn(m1, 1), turn(m2, 2), turn(m3, 3)
    far = swap(jnp.concatenate([m0[16:], l1[16:], l2[16:], l3[16:]], axis=0))
    lists = (pos, m0, l1, l2, l3, far)
    lm = [sm] + [vm] * 5
    h_fwd, h_bwd, inv, h_flag = call(
        k_boundary, (shape((256, 1024), BF16), shape((1024, 256), BF16), block, shape((1,), I32)),
        (own_to, halo_to, halo_from, hub_to), flops=1 << 31,
    )
    fwd, flag = call(k_fwd, (shape((8, 256, 512), BF16), shape((1,), I32)), lists, lm, flops=1 << 31)
    bwd = call(k_bwd, shape((8, 512, 256), BF16), lists, lm, flops=1 << 31)
    part = call(k_partial, [block] * 8, (flag, *lists, features, incoming, fwd), [sm, *lm, vm, vm, vm])
    other = part[4] + turn(part[5], 1) + turn(part[7], 3) + turn(part[6], 2)
    other, p1, p2, p3 = lax.optimization_barrier((other, part[1], part[2], part[3]))
    other = swap(other)
    near = [turn(p1, 1), turn(p3, 3), turn(p2, 2)]
    own = call(k_halo, block, (h_flag, halo_to, halo_from, incoming, h_fwd, part[0]), [sm] + [vm] * 5)
    inv, bwd = lax.optimization_barrier((inv, bwd))
    output, grad_pre, grad_sum, mean = call(
        k_layer, [block] * 4, (own, other, *near, inv, features, w_neigh, w_root, bias.reshape(1, 128), grad_out),
    )
    g4 = swap(grad_sum)
    g1, g3, g2 = turn(grad_sum, 3), turn(grad_sum, 1), turn(grad_sum, 2)
    weights = exchange(call(k_weights, shape((32, 16, 128)), (grad_pre, mean, features)), "grp")
    slots, root = call(
        k_slots, [shape((1024, 128)), block], (h_flag, halo_to, halo_from, grad_sum, h_bwd, grad_pre, w_root),
        [sm] + [vm] * 6,
    )
    g5, g7, g6 = turn(g4, 3), turn(g4, 1), turn(g4, 2)
    w = call(k_sum, shape((16, 128)), (weights,))
    w = w + turn(w, 1) + turn(w, 2) + turn(w, 3)
    w_far = swap(w)
    local, hubs = call(
        k_back, [block, shape((32, 8, 128))],
        (flag, *lists, grad_sum, g1, g2, g3, g4, g5, g6, g7, bwd, root), [sm, *lm] + [vm] * 10,
        [pltpu.VMEM((512, 128), F32)],
    )
    factor = (256 * lax.axis_size("grp") * lax.axis_size("blk")) ** (-0.5)
    back, grad_bias = call(
        functools.partial(k_pack, factor), [shape((32, 48, 128)), shape((1, 128))], (slots, hubs, w, w_far)
    )
    returned = exchange(back, "grp")
    grad_features, grad_wn, grad_wr = call(
        k_final, [block, shape((128, 128)), shape((128, 128))], (returned, send, hub, local), [vm, vm, sm, vm]
    )
    return output, grad_features, grad_wn, grad_wr, grad_bias.reshape(128)


def solution(mesh):
    rows = P(("grp", "blk"), None)
    in_specs = (
        rows, P(), P(), P(), rows,
        P("grp", "blk", None, None, None),
        P("grp", "blk", None, None, None, None),
        P("grp", "blk", None, None),
        P("grp", "blk", None), P("grp", "blk", None), P("grp", "blk", None), P("grp", "blk", None), P("grp", "blk", None),
    )
    return jax.shard_map(
        per_device, mesh=mesh, in_specs=in_specs, out_specs=(rows, rows, P(), P(), P()), check_vma=False
    )
```

```python
import functools

import jax
import jax.numpy as jnp
from jax import lax
from jax.experimental import pallas as pl
from jax.experimental.pallas import tpu as pltpu
from jax.sharding import PartitionSpec as P

HIGH = lax.Precision.HIGHEST
F32, BF16, I32 = jnp.float32, jnp.bfloat16, jnp.int32
NT = (((1,), (1,)), ((), ()))
NN = (((1,), (0,)), ((), ()))
TN = (((0,), (0,)), ((), ()))


def dot(a, b, dims=NN, precision=None):
    return lax.dot_general(a, b, dims, precision=precision, preferred_element_type=F32)


def halves(x):
    high = x.astype(BF16)
    low = (x - high.astype(F32)).astype(BF16)
    return jnp.concatenate([high, low], axis=1)


def joined(y):
    n = y.shape[1] // 2
    return y[:, :n] + y[:, n:]


def one_hot(idx, rows):
    n = idx.shape[1]
    row = lax.broadcasted_iota(I32, (rows, n), 0)
    return jnp.where(row == idx, 1.0, 0.0).astype(BF16)


def lanes(ref_rows):
    return jnp.concatenate(ref_rows, axis=1)


def call(kernel, out_shape, args, specs=None, scratch=(), flops=1 << 28):
    whole = pl.BlockSpec(memory_space=pltpu.VMEM)
    size = sum(int(a.size) * a.dtype.itemsize for a in args)
    return pl.pallas_call(
        kernel,
        out_shape=out_shape,
        in_specs=[whole] * len(args) if specs is None else specs,
        out_specs=jax.tree.map(
            lambda s: pl.BlockSpec(memory_space=pltpu.SMEM if s.shape == (1,) else pltpu.VMEM), out_shape
        ),
        scratch_shapes=list(scratch),
        compiler_params=pltpu.CompilerParams(vmem_limit_bytes=16 << 20),
        cost_estimate=pl.CostEstimate(flops=flops, bytes_accessed=size, transcendentals=0),
    )(*args)


def shape(s, d=F32):
    return jax.ShapeDtypeStruct(s, d)


def expm1(x):
    series = x * (1 + x * (1 / 2) * (1 + x * (1 / 3) * (1 + x * (1 / 4) * (1 + x * (1 / 5) * (1 + x * (1 / 6) * (1 + x * (1 / 7)))))))
    return jnp.where(x > -0.35, series, jnp.exp(x) - 1.0)


def send_hot(send):
    return lanes([one_hot(lanes([send[4 * i + j : 4 * i + j + 1, :] for j in range(4)]), 256) for i in range(8)])


def k_send(features, send, hub, out):
    x = halves(features[...])
    rows = joined(dot(send_hot(send), x, TN))
    out[:, 0:32, :] = rows.reshape(32, 32, 128)
    hub_rows = joined(dot(one_hot(hub[...], 256), x, TN))
    for p in range(32):
        out[p, 32:40, :] = hub_rows


def k_lists(pos, coord, edge, hub_to, hub_from, own_to, *outs):
    me = pos[0]
    for b in range(8):
        for t in range(6):
            own_to[b * 6 + t : b * 6 + t + 1, :] = edge[b, t, 0:1, :] + coord[b, 0, t] * 128
    for d in range(2):
        for k in range(4):
            b = jnp.bitwise_xor(me // 4, d) * 4 + (me % 4 + k) % 4
            at = d * 16
            for t in range(6):
                outs[k][at + t : at + t + 1, :] = edge[b, t, 0:1, :] + coord[b, 0, t] * 128
                outs[k][at + 6 + t : at + 7 + t, :] = edge[b, t, 1:2, :] + coord[b, 1, t] * 128
            outs[k][at + 12 : at + 14, :] = hub_to[...]
            outs[k][at + 14 : at + 16, :] = hub_from[...]


def hots(pos, block):
    me = pos[0]
    to = lanes([one_hot(block[i : i + 1, :], 256) for i in range(6)])
    frm = lanes([one_hot(block[i : i + 1, :], 256) for i in range(6, 12)])
    h_to = lanes([one_hot(block[i : i + 1, :], 256) for i in range(12, 14)])
    codes = [block[i : i + 1, :] for i in range(14, 16)]
    rows = [jnp.where((c >> 3) % 8 == me, (c >> 6) * 8 + c % 8, -1) for c in codes]
    return to, frm, h_to, lanes([one_hot(c, 256) for c in rows])


def blocks_of(lists):
    own, l1, l2, l3, far = lists
    return [ref[0:16, :] for ref in (own, l1, l2, l3)] + [far[16 * k : 16 * k + 16, :] for k in range(4)]


def halo_hots(halo_to, halo_from):
    to = lanes([one_hot(halo_to[i : i + 1, :], 256) for i in range(8)])
    return to, lanes([one_hot(halo_from[i : i + 1, :], 1024) for i in range(8)])


def rest(count):
    return (count - count.astype(BF16).astype(F32)).astype(BF16)


def forward_count(to, frm, h_to, h_frm):
    return jnp.concatenate([dot(to, frm, NT), dot(h_to, h_frm, NT)], axis=1)


def backward_count(to, frm, h_to, h_frm):
    return jnp.concatenate([dot(frm, to, NT), dot(h_frm, h_to, NT)], axis=0)


def k_fwd(pos, l0, l1, l2, l3, far, fwd, flag):
    top = jnp.float32(0.0)
    for r, block in enumerate(blocks_of((l0, l1, l2, l3, far))):
        count = forward_count(*hots(pos, block))
        top = jnp.maximum(top, jnp.max(count))
        fwd[r] = count.astype(BF16)
    flag[0] = (top > 256.0).astype(I32)


def k_bwd(pos, l0, l1, l2, l3, far, bwd):
    for r, block in enumerate(blocks_of((l0, l1, l2, l3, far))):
        bwd[r] = backward_count(*hots(pos, block)).astype(BF16)


def k_boundary(own_to, halo_to, halo_from, hub_to, h_fwd, h_bwd, inv, flag):
    to, frm = halo_hots(halo_to, halo_from)
    count = dot(to, frm, NT)
    h_fwd[...] = count.astype(BF16)
    h_bwd[...] = dot(frm, to, NT).astype(BF16)
    flag[0] = (jnp.max(count) > 256.0).astype(I32)
    row = lax.broadcasted_iota(I32, (256, 128), 0)
    degree = jnp.zeros((256, 128), F32)
    for ref, n in ((own_to, 48), (halo_to, 8), (hub_to, 2)):
        for i in range(n):
            degree = degree + jnp.where(row == ref[i : i + 1, :], 1.0, 0.0)
    degree = jnp.sum(degree, axis=1, keepdims=True)
    inv[...] = jnp.broadcast_to(1.0 / (degree + 1.0), (256, 128))


def k_partial(flag, pos, l0, l1, l2, l3, far, features, incoming, fwd, *outs):
    hubs = incoming[:, 32:40, :].reshape(256, 128)
    x = jnp.concatenate([halves(features[...]), halves(hubs)], axis=0)
    for r in range(8):
        outs[r][...] = joined(dot(fwd[r], x))

    @pl.when(flag[0] != 0)
    def _():
        for r, block in enumerate(blocks_of((l0, l1, l2, l3, far))):
            outs[r][...] += joined(dot(rest(forward_count(*hots(pos, block))), x))


def k_halo(flag, halo_to, halo_from, incoming, h_fwd, own, out):
    x = halves(incoming[:, 0:32, :].reshape(1024, 128))
    out[...] = own[...] + joined(dot(h_fwd[...], x))

    @pl.when(flag[0] != 0)
    def _():
        to, frm = halo_hots(halo_to, halo_from)
        out[...] += joined(dot(rest(dot(to, frm, NT)), x))


def k_layer(a0, a1, a2, a3, a4, inv, features, w_neigh, w_root, bias, grad_out,
            output, grad_pre, grad_sum, mean):
    scale = inv[...]
    m = (a0[...] + a1[...] + a2[...] + a3[...] + a4[...]) * scale
    mean[...] = m
    pre = dot(m, w_neigh[...], NN, HIGH) + dot(features[...], w_root[...], NN, HIGH) + bias[...]
    negative = jnp.minimum(pre, 0.0)
    output[...] = jnp.where(pre > 0, pre, expm1(negative))
    g = grad_out[...] * jnp.where(pre > 0, 1.0, jnp.exp(negative))
    grad_pre[...] = g
    grad_sum[...] = dot(g, w_neigh[...], NT, HIGH) * scale


def k_weights(grad_pre, mean, features, out):
    g = grad_pre[...]
    out[0:16, 0:8, :] = dot(mean[...], g, TN, HIGH).reshape(16, 8, 128)
    out[16:32, 0:8, :] = dot(features[...], g, TN, HIGH).reshape(16, 8, 128)
    fill = jnp.broadcast_to(jnp.sum(g, axis=0, keepdims=True), (8, 128))
    for p in range(32):
        out[p, 8:16, :] = fill


def k_slots(flag, halo_to, halo_from, grad_sum, h_bwd, grad_pre, w_root, out, root):
    x = halves(grad_sum[...])
    out[...] = joined(dot(h_bwd[...], x))
    root[...] = dot(grad_pre[...], w_root[...], NT, HIGH)

    @pl.when(flag[0] != 0)
    def _():
        to, frm = halo_hots(halo_to, halo_from)
        out[...] += joined(dot(rest(dot(frm, to, NT)), x))


def k_back(flag, pos, l0, l1, l2, l3, far, g0, g1, g2, g3, g4, g5, g6, g7, bwd, root, slots, local, out, total):
    xs = [halves(g[...]) for g in (g0, g1, g2, g3, g4, g5, g6, g7)]
    acc = dot(bwd[0], xs[0])
    for r in range(1, 8):
        acc = acc + dot(bwd[r], xs[r])
    total[...] = joined(acc)

    @pl.when(flag[0] != 0)
    def _():
        for r, block in enumerate(blocks_of((l0, l1, l2, l3, far))):
            total[...] += joined(dot(rest(backward_count(*hots(pos, block))), xs[r]))

    out[:, 0:32, :] = slots[...].reshape(32, 32, 128)
    out[:, 32:40, :] = total[256:512, :].reshape(32, 8, 128)
    local[...] = root[...] + total[0:256, :]


def k_sum(weights, out):
    out[...] = jnp.sum(weights[...], axis=0)


def k_scale(factor, near, far, out, bias):
    w = (near[...] + far[...]) * factor
    out[...] = w[0:8]
    bias[...] = w[8:9]


def k_place(here, a, b, w_neigh, w_root, held):
    g = here[0]
    zl, x, c = g // 8, g // 2 % 4, g % 2
    for d, ref in enumerate((a, b)):
        for k in range(4):
            for m in range(4):
                at = (jnp.bitwise_xor(zl, m) * 4 + (x + 4 - k) % 4) * 2 + jnp.bitwise_xor(c, d)
                held[pl.ds(pl.multiple_of(at * 8, 8), 8), :] = ref[k * 32 + m * 8 : k * 32 + m * 8 + 8, :]
    w_neigh[...] = held[0:128, :]
    w_root[...] = held[128:256, :]


def k_final(returned, send, hub, local, out):
    acc = joined(dot(send_hot(send), halves(returned[:, 0:32, :].reshape(1024, 128))))
    rows = jnp.sum(returned[:, 32:40, :], axis=0)
    out[...] = local[...] + acc
    for j in range(8):
        out[pl.ds(hub[j], 1), :] += rows[j : j + 1, :]


def per_device(features, w_neigh, w_root, bias, grad_out, tile_coord, tile_edge,
               send_idx, halo_dst, halo_src, hub_idx, hub_dst, hub_src):
    send = send_idx.reshape(32, 32)
    hub = hub_idx.reshape(8)
    hub_to = hub_dst.reshape(2, 128)
    hub_from = hub_src.reshape(2, 128)
    halo_to = halo_dst.reshape(8, 128)
    halo_from = halo_src.reshape(8, 128)
    pos = lax.axis_index("blk").astype(I32).reshape(1)
    block = shape((256, 128))

    def swap(v):
        return lax.ppermute(v, "blk", [(i, i ^ 4) for i in range(8)])

    def turn(v, k):
        return lax.ppermute(v, "blk", [(i, i // 4 * 4 + (i % 4 + k) % 4) for i in range(8)])

    def exchange(v, axis):
        return lax.all_to_all(v, axis, split_axis=0, concat_axis=0, tiled=True)

    vm, sm = (pl.BlockSpec(memory_space=s) for s in (pltpu.VMEM, pltpu.SMEM))

    outgoing = call(k_send, shape((32, 40, 128)), (features, send, hub_idx.reshape(1, 8)))
    outgoing, coord = lax.optimization_barrier((outgoing, tile_coord.reshape(8, 2, 6)))
    incoming = exchange(outgoing, "grp")
    own_to, m0, m1, m2, m3 = call(
        k_lists, [shape((48, 128), I32)] + [shape((32, 128), I32)] * 4,
        (pos, coord, tile_edge.reshape(8, 6, 2, 128), hub_to, hub_from), [sm, sm, vm, vm, vm],
    )
    l3, l2, l1 = turn(m1, 1), turn(m2, 2), turn(m3, 3)
    far = swap(jnp.concatenate([m0[16:], l1[16:], l2[16:], l3[16:]], axis=0))
    lists = (pos, m0, l1, l2, l3, far)
    lm = [sm] + [vm] * 5
    h_fwd, h_bwd, inv, h_flag = call(
        k_boundary, (shape((256, 1024), BF16), shape((1024, 256), BF16), block, shape((1,), I32)),
        (own_to, halo_to, halo_from, hub_to), flops=1 << 31,
    )
    fwd, flag = call(k_fwd, (shape((8, 256, 512), BF16), shape((1,), I32)), lists, lm, flops=1 << 31)
    bwd = call(k_bwd, shape((8, 512, 256), BF16), lists, lm, flops=1 << 31)
    part = call(k_partial, [block] * 8, (flag, *lists, features, incoming, fwd), [sm, *lm, vm, vm, vm])
    other = part[4] + turn(part[5], 1) + turn(part[7], 3) + turn(part[6], 2)
    other, p1, p2, p3 = lax.optimization_barrier((other, part[1], part[2], part[3]))
    other = swap(other)
    near = [turn(p1, 1), turn(p3, 3), turn(p2, 2)]
    own = call(k_halo, block, (h_flag, halo_to, halo_from, incoming, h_fwd, part[0]), [sm] + [vm] * 5)
    inv, bwd = lax.optimization_barrier((inv, bwd))
    output, grad_pre, grad_sum, mean = call(
        k_layer, [block] * 4, (own, other, *near, inv, features, w_neigh, w_root, bias.reshape(1, 128), grad_out),
    )
    g4 = swap(grad_sum)
    g1, g3, g2 = turn(grad_sum, 3), turn(grad_sum, 1), turn(grad_sum, 2)
    weights = exchange(call(k_weights, shape((32, 16, 128)), (grad_pre, mean, features)), "grp")
    slots, root = call(
        k_slots, [shape((1024, 128)), block], (h_flag, halo_to, halo_from, grad_sum, h_bwd, grad_pre, w_root),
        [sm] + [vm] * 6,
    )
    g5, g7, g6 = turn(g4, 3), turn(g4, 1), turn(g4, 2)
    local, back = call(
        k_back, [block, shape((32, 40, 128))],
        (flag, *lists, grad_sum, g1, g2, g3, g4, g5, g6, g7, bwd, root, slots), [sm, *lm] + [vm] * 11,
        [pltpu.VMEM((512, 128), F32)],
    )
    returned = exchange(back, "grp")
    back, weights = lax.optimization_barrier((back, weights))
    w = call(k_sum, shape((16, 128)), (weights,))
    w = w + turn(w, 1) + turn(w, 2) + turn(w, 3)
    factor = (256 * lax.axis_size("grp") * lax.axis_size("blk")) ** (-0.5)
    w, grad_bias = call(functools.partial(k_scale, factor), [shape((8, 128)), shape((1, 128))], (w, swap(w)))
    w = jnp.concatenate([w] + [lax.ppermute(w, "grp", [(i, i ^ (8 * m)) for i in range(32)]) for m in (1, 2, 3)], axis=0)
    spin = [
        lax.ppermute(w, "grp", [(i, i // 8 * 8 + (i % 8 + 2 * k) % 8) for i in range(32)]) for k in (1, 2, 3)
    ]
    w = jnp.concatenate([w] + spin, axis=0)
    w_core = lax.ppermute(w, "grp", [(i, i ^ 1) for i in range(32)])
    here = lax.axis_index("grp").astype(I32).reshape(1)
    grad_wn, grad_wr = call(
        k_place, [shape((128, 128))] * 2, (here, w, w_core), [sm, vm, vm], [pltpu.VMEM((256, 128), F32)]
    )
    grad_features = call(k_final, block, (returned, send, hub, local), [vm, vm, sm, vm])
    return output, grad_features, grad_wn, grad_wr, grad_bias.reshape(128)


def solution(mesh):
    rows = P(("grp", "blk"), None)
    in_specs = (
        rows, P(), P(), P(), rows,
        P("grp", "blk", None, None, None),
        P("grp", "blk", None, None, None, None),
        P("grp", "blk", None, None),
        P("grp", "blk", None), P("grp", "blk", None), P("grp", "blk", None), P("grp", "blk", None), P("grp", "blk", None),
    )
    return jax.shard_map(
        per_device, mesh=mesh, in_specs=in_specs, out_specs=(rows, rows, P(), P(), P()), check_vma=False
    )
```

```python
import functools

import jax
import jax.numpy as jnp
from jax import lax
from jax.experimental import pallas as pl
from jax.experimental.pallas import tpu as pltpu
from jax.sharding import PartitionSpec as P

HIGH = lax.Precision.HIGHEST
F32, BF16, I32 = jnp.float32, jnp.bfloat16, jnp.int32
NT = (((1,), (1,)), ((), ()))
NN = (((1,), (0,)), ((), ()))
TN = (((0,), (0,)), ((), ()))


def dot(a, b, dims=NN, precision=None):
    return lax.dot_general(a, b, dims, precision=precision, preferred_element_type=F32)


def halves(x):
    high = x.astype(BF16)
    low = (x - high.astype(F32)).astype(BF16)
    return jnp.concatenate([high, low], axis=1)


def joined(y):
    n = y.shape[1] // 2
    return y[:, :n] + y[:, n:]


def one_hot(idx, rows):
    n = idx.shape[1]
    row = lax.broadcasted_iota(I32, (rows, n), 0)
    return jnp.where(row == idx, 1.0, 0.0).astype(BF16)


def lanes(ref_rows):
    return jnp.concatenate(ref_rows, axis=1)


def call(kernel, out_shape, args, specs=None, scratch=(), flops=1 << 28, limit=16 << 20):
    whole = pl.BlockSpec(memory_space=pltpu.VMEM)
    size = sum(int(a.size) * a.dtype.itemsize for a in args)
    return pl.pallas_call(
        kernel,
        out_shape=out_shape,
        in_specs=[whole] * len(args) if specs is None else specs,
        out_specs=jax.tree.map(
            lambda s: pl.BlockSpec(memory_space=pltpu.SMEM if s.shape == (1,) else pltpu.VMEM), out_shape
        ),
        scratch_shapes=list(scratch),
        compiler_params=pltpu.CompilerParams(vmem_limit_bytes=limit),
        cost_estimate=pl.CostEstimate(flops=flops, bytes_accessed=size, transcendentals=0),
    )(*args)


def shape(s, d=F32):
    return jax.ShapeDtypeStruct(s, d)


def expm1(x):
    series = x * (1 + x * (1 / 2) * (1 + x * (1 / 3) * (1 + x * (1 / 4) * (1 + x * (1 / 5) * (1 + x * (1 / 6) * (1 + x * (1 / 7)))))))
    return jnp.where(x > -0.35, series, jnp.exp(x) - 1.0)


def send_hot(send):
    return lanes([one_hot(lanes([send[4 * i + j : 4 * i + j + 1, :] for j in range(4)]), 256) for i in range(8)])


def k_send(features_hbm, send_hbm, hub_hbm, out, features, send, hub, sems):
    pairs = ((features_hbm, features), (send_hbm, send), (hub_hbm, hub))
    copies = [pltpu.make_async_copy(src, dst, sems.at[n]) for n, (src, dst) in enumerate(pairs)]
    for copy in copies:
        copy.start()
    for copy in copies:
        copy.wait()
    x = halves(features[...])
    out[:, 0:32, :] = joined(dot(send_hot(send), x, TN)).reshape(32, 32, 128)
    hub_rows = joined(dot(one_hot(hub[...], 256), x, TN))
    for p in range(32):
        out[p, 32:40, :] = hub_rows


def k_lists(pos, coord, edge, hub_to, hub_from, own_to, *outs):
    me = pos[0]
    for b in range(8):
        for t in range(6):
            own_to[b * 6 + t : b * 6 + t + 1, :] = edge[b, t, 0:1, :] + coord[b, 0, t] * 128
    for d in range(2):
        for k in range(4):
            b = jnp.bitwise_xor(me // 4, d) * 4 + (me % 4 + k) % 4
            at = d * 16
            for t in range(6):
                outs[k][at + t : at + t + 1, :] = edge[b, t, 0:1, :] + coord[b, 0, t] * 128
                outs[k][at + 6 + t : at + 7 + t, :] = edge[b, t, 1:2, :] + coord[b, 1, t] * 128
            outs[k][at + 12 : at + 14, :] = hub_to[...]
            outs[k][at + 14 : at + 16, :] = hub_from[...]


def hots(pos, block):
    me = pos[0]
    to = lanes([one_hot(block[i : i + 1, :], 256) for i in range(6)])
    frm = lanes([one_hot(block[i : i + 1, :], 256) for i in range(6, 12)])
    h_to = lanes([one_hot(block[i : i + 1, :], 256) for i in range(12, 14)])
    codes = [block[i : i + 1, :] for i in range(14, 16)]
    rows = [jnp.where((c >> 3) % 8 == me, (c >> 6) * 8 + c % 8, -1) for c in codes]
    return to, frm, h_to, lanes([one_hot(c, 256) for c in rows])


def blocks_of(lists):
    own, l1, l2, l3, far = lists
    return [ref[0:16, :] for ref in (own, l1, l2, l3)] + [far[16 * k : 16 * k + 16, :] for k in range(4)]


def halo_hots(halo_to, halo_from):
    to = lanes([one_hot(halo_to[i : i + 1, :], 256) for i in range(8)])
    return to, lanes([one_hot(halo_from[i : i + 1, :], 1024) for i in range(8)])


def rest(count):
    return (count - count.astype(BF16).astype(F32)).astype(BF16)


def forward_count(to, frm, h_to, h_frm):
    return jnp.concatenate([dot(to, frm, NT), dot(h_to, h_frm, NT)], axis=1)


def backward_count(to, frm, h_to, h_frm):
    return jnp.concatenate([dot(frm, to, NT), dot(h_frm, h_to, NT)], axis=0)


def k_fwd(pos, l0, l1, l2, l3, far, fwd, flag):
    top = jnp.float32(0.0)
    for r, block in enumerate(blocks_of((l0, l1, l2, l3, far))):
        count = forward_count(*hots(pos, block))
        top = jnp.maximum(top, jnp.max(count))
        fwd[r] = count.astype(BF16)
    flag[0] = (top > 256.0).astype(I32)


def k_bwd(pos, l0, l1, l2, l3, far, bwd):
    for r, block in enumerate(blocks_of((l0, l1, l2, l3, far))):
        bwd[r] = backward_count(*hots(pos, block)).astype(BF16)


def k_boundary(own_to, halo_to, halo_from, hub_to, h_fwd, h_bwd, inv, flag):
    to, frm = halo_hots(halo_to, halo_from)
    count = dot(to, frm, NT)
    h_fwd[...] = count.astype(BF16)
    h_bwd[...] = dot(frm, to, NT).astype(BF16)
    flag[0] = (jnp.max(count) > 256.0).astype(I32)
    row = lax.broadcasted_iota(I32, (256, 128), 0)
    degree = jnp.zeros((256, 128), F32)
    for ref, n in ((own_to, 48), (halo_to, 8), (hub_to, 2)):
        for i in range(n):
            degree = degree + jnp.where(row == ref[i : i + 1, :], 1.0, 0.0)
    degree = jnp.sum(degree, axis=1, keepdims=True)
    inv[...] = jnp.broadcast_to(1.0 / (degree + 1.0), (256, 128))


def k_partial(flag, pos, l0, l1, l2, l3, far, features, incoming, fwd, *outs):
    hubs = incoming[:, 32:40, :].reshape(256, 128)
    x = jnp.concatenate([halves(features[...]), halves(hubs)], axis=0)
    for r in range(8):
        outs[r][...] = joined(dot(fwd[r], x))

    @pl.when(flag[0] != 0)
    def _():
        for r, block in enumerate(blocks_of((l0, l1, l2, l3, far))):
            outs[r][...] += joined(dot(rest(forward_count(*hots(pos, block))), x))


def k_halo(flag, halo_to, halo_from, incoming, h_fwd, own, out):
    x = halves(incoming[:, 0:32, :].reshape(1024, 128))
    out[...] = own[...] + joined(dot(h_fwd[...], x))

    @pl.when(flag[0] != 0)
    def _():
        to, frm = halo_hots(halo_to, halo_from)
        out[...] += joined(dot(rest(dot(to, frm, NT)), x))


def k_layer(a0, a1, a2, a3, a4, inv, features, w_neigh, w_root, bias, grad_out,
            output, grad_pre, grad_sum, mean):
    scale = inv[...]
    m = (a0[...] + a1[...] + a2[...] + a3[...] + a4[...]) * scale
    mean[...] = m
    pre = dot(m, w_neigh[...], NN, HIGH) + dot(features[...], w_root[...], NN, HIGH) + bias[...]
    negative = jnp.minimum(pre, 0.0)
    output[...] = jnp.where(pre > 0, pre, expm1(negative))
    g = grad_out[...] * jnp.where(pre > 0, 1.0, jnp.exp(negative))
    grad_pre[...] = g
    grad_sum[...] = dot(g, w_neigh[...], NT, HIGH) * scale


def k_weights(grad_pre, mean, features, out):
    g = grad_pre[...]
    out[0:16, 0:8, :] = dot(mean[...], g, TN, HIGH).reshape(16, 8, 128)
    out[16:32, 0:8, :] = dot(features[...], g, TN, HIGH).reshape(16, 8, 128)
    fill = jnp.broadcast_to(jnp.sum(g, axis=0, keepdims=True), (8, 128))
    for p in range(32):
        out[p, 8:16, :] = fill


def k_slots(flag, halo_to, halo_from, grad_sum, h_bwd, grad_pre, w_root, out, root):
    x = halves(grad_sum[...])
    out[...] = joined(dot(h_bwd[...], x))
    root[...] = dot(grad_pre[...], w_root[...], NT, HIGH)

    @pl.when(flag[0] != 0)
    def _():
        to, frm = halo_hots(halo_to, halo_from)
        out[...] += joined(dot(rest(dot(frm, to, NT)), x))


def k_back(flag, pos, l0, l1, l2, l3, far, g0, g1, g2, g3, g4, g5, g6, g7, bwd, root, local, hubs, total):
    xs = [halves(g[0:256, :]) for g in (g0, g1, g2, g3, g4, g5, g6, g7)]
    acc = dot(bwd[0], xs[0])
    for r in range(1, 8):
        acc = acc + dot(bwd[r], xs[r])
    total[...] = joined(acc)

    @pl.when(flag[0] != 0)
    def _():
        for r, block in enumerate(blocks_of((l0, l1, l2, l3, far))):
            total[...] += joined(dot(rest(backward_count(*hots(pos, block))), xs[r]))

    hubs[...] = total[256:512, :].reshape(32, 8, 128)
    local[...] = root[...] + total[0:256, :]


def k_join(grad, weights, out):
    out[0:256, :] = grad[...]
    out[256:272, :] = jnp.sum(weights[...], axis=0)


def k_sum(a, b, c, d, out):
    out[...] = a[256:272, :] + b[256:272, :] + c[256:272, :] + d[256:272, :]


def k_pack(factor, slots, hubs, near, far, out, bias):
    w = (near[...] + far[...]) * factor
    out[:, 0:32, :] = slots[...].reshape(32, 32, 128)
    out[:, 32:40, :] = hubs[...]
    for p in range(32):
        out[p, 40:48, :] = w[0:8]
    bias[...] = w[8:9]


def k_final(returned, send, hub, local, out, w_neigh, w_root):
    acc = joined(dot(send_hot(send), halves(returned[:, 0:32, :].reshape(1024, 128))))
    rows = jnp.sum(returned[:, 32:40, :], axis=0)
    out[...] = local[...] + acc
    for j in range(8):
        out[pl.ds(hub[j], 1), :] += rows[j : j + 1, :]
    w_neigh[...] = returned[0:16, 40:48, :].reshape(128, 128)
    w_root[...] = returned[16:32, 40:48, :].reshape(128, 128)


def per_device(features, w_neigh, w_root, bias, grad_out, tile_coord, tile_edge,
               send_idx, halo_dst, halo_src, hub_idx, hub_dst, hub_src):
    send = send_idx.reshape(32, 32)
    hub = hub_idx.reshape(8)
    hub_to = hub_dst.reshape(2, 128)
    hub_from = hub_src.reshape(2, 128)
    halo_to = halo_dst.reshape(8, 128)
    halo_from = halo_src.reshape(8, 128)
    pos = lax.axis_index("blk").astype(I32).reshape(1)
    block = shape((256, 128))

    def swap(v):
        return lax.ppermute(v, "blk", [(i, i ^ 4) for i in range(8)])

    def turn(v, k):
        return lax.ppermute(v, "blk", [(i, i // 4 * 4 + (i % 4 + k) % 4) for i in range(8)])

    def exchange(v, axis):
        return lax.all_to_all(v, axis, split_axis=0, concat_axis=0, tiled=True)

    vm, sm, hb = (pl.BlockSpec(memory_space=s) for s in (pltpu.VMEM, pltpu.SMEM, pltpu.HBM))

    outgoing = call(
        k_send, shape((32, 40, 128)), (features, send, hub_idx.reshape(1, 8)), [hb] * 3,
        [pltpu.VMEM((256, 128), F32), pltpu.VMEM((32, 32), I32), pltpu.VMEM((1, 8), I32), pltpu.SemaphoreType.DMA((3,))],
        limit=60 << 20,
    )
    outgoing, coord = lax.optimization_barrier((outgoing, tile_coord.reshape(8, 2, 6)))
    incoming = exchange(outgoing, "grp")
    own_to, m0, m1, m2, m3 = call(
        k_lists, [shape((48, 128), I32)] + [shape((32, 128), I32)] * 4,
        (pos, coord, tile_edge.reshape(8, 6, 2, 128), hub_to, hub_from), [sm, sm, vm, vm, vm],
    )
    l3, l2, l1 = turn(m1, 1), turn(m2, 2), turn(m3, 3)
    far = swap(jnp.concatenate([m0[16:], l1[16:], l2[16:], l3[16:]], axis=0))
    lists = (pos, m0, l1, l2, l3, far)
    lm = [sm] + [vm] * 5
    h_fwd, h_bwd, inv, h_flag = call(
        k_boundary, (shape((256, 1024), BF16), shape((1024, 256), BF16), block, shape((1,), I32)),
        (own_to, halo_to, halo_from, hub_to), flops=1 << 31,
    )
    fwd, flag = call(k_fwd, (shape((8, 256, 512), BF16), shape((1,), I32)), lists, lm, flops=1 << 31)
    bwd = call(k_bwd, shape((8, 512, 256), BF16), lists, lm, flops=1 << 31)
    part = call(k_partial, [block] * 8, (flag, *lists, features, incoming, fwd), [sm, *lm, vm, vm, vm])
    other = part[4] + turn(part[5], 1) + turn(part[7], 3) + turn(part[6], 2)
    other, p1, p2, p3 = lax.optimization_barrier((other, part[1], part[2], part[3]))
    other = swap(other)
    near = [turn(p1, 1), turn(p3, 3), turn(p2, 2)]
    own = call(k_halo, block, (h_flag, halo_to, halo_from, incoming, h_fwd, part[0]), [sm] + [vm] * 5)
    inv, bwd = lax.optimization_barrier((inv, bwd))
    output, grad_pre, grad_sum, mean = call(
        k_layer, [block] * 4, (own, other, *near, inv, features, w_neigh, w_root, bias.reshape(1, 128), grad_out),
    )
    g4 = swap(grad_sum)
    g1, g3, g2 = turn(grad_sum, 3), turn(grad_sum, 1), turn(grad_sum, 2)
    weights = exchange(call(k_weights, shape((32, 16, 128)), (grad_pre, mean, features)), "grp")
    slots, root = call(
        k_slots, [shape((1024, 128)), block], (h_flag, halo_to, halo_from, grad_sum, h_bwd, grad_pre, w_root),
        [sm] + [vm] * 6,
    )
    g4, weights, g1, g2, g3, slots = lax.optimization_barrier((g4, weights, g1, g2, g3, slots))
    g4 = call(k_join, shape((272, 128)), (g4, weights))
    g5, g7, g6 = turn(g4, 3), turn(g4, 1), turn(g4, 2)
    w = call(k_sum, shape((16, 128)), (g4, g5, g6, g7))
    w_far = swap(w)
    local, hubs = call(
        k_back, [block, shape((32, 8, 128))],
        (flag, *lists, grad_sum, g1, g2, g3, g4, g5, g6, g7, bwd, root), [sm, *lm] + [vm] * 10,
        [pltpu.VMEM((512, 128), F32)],
    )
    factor = (256 * lax.axis_size("grp") * lax.axis_size("blk")) ** (-0.5)
    back, grad_bias = call(
        functools.partial(k_pack, factor), [shape((32, 48, 128)), shape((1, 128))], (slots, hubs, w, w_far)
    )
    returned = exchange(back, "grp")
    grad_features, grad_wn, grad_wr = call(
        k_final, [block, shape((128, 128)), shape((128, 128))], (returned, send, hub, local), [vm, vm, sm, vm]
    )
    return output, grad_features, grad_wn, grad_wr, grad_bias.reshape(128)


def solution(mesh):
    rows = P(("grp", "blk"), None)
    in_specs = (
        rows, P(), P(), P(), rows,
        P("grp", "blk", None, None, None),
        P("grp", "blk", None, None, None, None),
        P("grp", "blk", None, None),
        P("grp", "blk", None), P("grp", "blk", None), P("grp", "blk", None), P("grp", "blk", None), P("grp", "blk", None),
    )
    return jax.shard_map(
        per_device, mesh=mesh, in_specs=in_specs, out_specs=(rows, rows, P(), P(), P()), check_vma=False
    )
```

```python
import functools

import jax
import jax.numpy as jnp
from jax import lax
from jax.experimental import pallas as pl
from jax.experimental.pallas import tpu as pltpu
from jax.sharding import PartitionSpec as P

HIGH = lax.Precision.HIGHEST
F32, BF16, I32 = jnp.float32, jnp.bfloat16, jnp.int32
NT = (((1,), (1,)), ((), ()))
NN = (((1,), (0,)), ((), ()))
TN = (((0,), (0,)), ((), ()))


def dot(a, b, dims=NN, precision=None):
    return lax.dot_general(a, b, dims, precision=precision, preferred_element_type=F32)


def halves(x):
    high = x.astype(BF16)
    low = (x - high.astype(F32)).astype(BF16)
    return jnp.concatenate([high, low], axis=1)


def joined(y):
    n = y.shape[1] // 2
    return y[:, :n] + y[:, n:]


def one_hot(idx, rows):
    n = idx.shape[1]
    row = lax.broadcasted_iota(I32, (rows, n), 0)
    return jnp.where(row == idx, 1.0, 0.0).astype(BF16)


def lanes(ref_rows):
    return jnp.concatenate(ref_rows, axis=1)


def call(kernel, out_shape, args, specs=None, scratch=(), flops=1 << 28, limit=16 << 20):
    whole = pl.BlockSpec(memory_space=pltpu.VMEM)
    size = sum(int(a.size) * a.dtype.itemsize for a in args)
    return pl.pallas_call(
        kernel,
        out_shape=out_shape,
        in_specs=[whole] * len(args) if specs is None else specs,
        out_specs=jax.tree.map(
            lambda s: pl.BlockSpec(memory_space=pltpu.SMEM if s.shape == (1,) else pltpu.VMEM), out_shape
        ),
        scratch_shapes=list(scratch),
        compiler_params=pltpu.CompilerParams(vmem_limit_bytes=limit),
        cost_estimate=pl.CostEstimate(flops=flops, bytes_accessed=size, transcendentals=0),
    )(*args)


def shape(s, d=F32):
    return jax.ShapeDtypeStruct(s, d)


def expm1(x):
    series = x * (1 + x * (1 / 2) * (1 + x * (1 / 3) * (1 + x * (1 / 4) * (1 + x * (1 / 5) * (1 + x * (1 / 6) * (1 + x * (1 / 7)))))))
    return jnp.where(x > -0.35, series, jnp.exp(x) - 1.0)


def send_hot(send):
    return lanes([one_hot(lanes([send[4 * i + j : 4 * i + j + 1, :] for j in range(4)]), 256) for i in range(8)])


def k_send(features_hbm, send_hbm, hub_hbm, out, features, send, hub, sems):
    pairs = ((features_hbm, features), (send_hbm, send), (hub_hbm, hub))
    copies = [pltpu.make_async_copy(src, dst, sems.at[n]) for n, (src, dst) in enumerate(pairs)]
    for copy in copies:
        copy.start()
    for copy in copies:
        copy.wait()
    x = halves(features[...])
    out[:, 0:32, :] = joined(dot(send_hot(send), x, TN)).reshape(32, 32, 128)
    hub_rows = joined(dot(one_hot(hub[...], 256), x, TN))
    for p in range(32):
        out[p, 32:40, :] = hub_rows


def k_lists(pos, coord, edge, hub_to, hub_from, own_to, *outs):
    me = pos[0]
    for b in range(8):
        for t in range(6):
            own_to[b * 6 + t : b * 6 + t + 1, :] = edge[b, t, 0:1, :] + coord[b, 0, t] * 128
    for d in range(2):
        for k in range(4):
            b = jnp.bitwise_xor(me // 4, d) * 4 + (me % 4 + k) % 4
            at = d * 16
            for t in range(6):
                outs[k][at + t : at + t + 1, :] = edge[b, t, 0:1, :] + coord[b, 0, t] * 128
                outs[k][at + 6 + t : at + 7 + t, :] = edge[b, t, 1:2, :] + coord[b, 1, t] * 128
            outs[k][at + 12 : at + 14, :] = hub_to[...]
            outs[k][at + 14 : at + 16, :] = hub_from[...]


def hots(pos, block):
    me = pos[0]
    to = lanes([one_hot(block[i : i + 1, :], 256) for i in range(6)])
    frm = lanes([one_hot(block[i : i + 1, :], 256) for i in range(6, 12)])
    h_to = lanes([one_hot(block[i : i + 1, :], 256) for i in range(12, 14)])
    codes = [block[i : i + 1, :] for i in range(14, 16)]
    rows = [jnp.where((c >> 3) % 8 == me, (c >> 6) * 8 + c % 8, -1) for c in codes]
    return to, frm, h_to, lanes([one_hot(c, 256) for c in rows])


def blocks_of(lists):
    own, l1, l2, l3, far = lists
    return [ref[0:16, :] for ref in (own, l1, l2, l3)] + [far[16 * k : 16 * k + 16, :] for k in range(4)]


def halo_hots(halo_to, halo_from):
    to = lanes([one_hot(halo_to[i : i + 1, :], 256) for i in range(8)])
    return to, lanes([one_hot(halo_from[i : i + 1, :], 1024) for i in range(8)])


def rest(count):
    return (count - count.astype(BF16).astype(F32)).astype(BF16)


def forward_count(to, frm, h_to, h_frm):
    return jnp.concatenate([dot(to, frm, NT), dot(h_to, h_frm, NT)], axis=1)


def backward_count(to, frm, h_to, h_frm):
    return jnp.concatenate([dot(frm, to, NT), dot(h_frm, h_to, NT)], axis=0)


def k_fwd(pos, l0, l1, l2, l3, far, fwd, flag):
    top = jnp.float32(0.0)
    for r, block in enumerate(blocks_of((l0, l1, l2, l3, far))):
        count = forward_count(*hots(pos, block))
        top = jnp.maximum(top, jnp.max(count))
        fwd[r] = count.astype(BF16)
    flag[0] = (top > 256.0).astype(I32)


def k_bwd(pos, l0, l1, l2, l3, far, bwd):
    for r, block in enumerate(blocks_of((l0, l1, l2, l3, far))):
        bwd[r] = backward_count(*hots(pos, block)).astype(BF16)


def k_boundary(own_to, halo_to, halo_from, hub_to, h_fwd, h_bwd, inv, flag):
    to, frm = halo_hots(halo_to, halo_from)
    count = dot(to, frm, NT)
    h_fwd[...] = count.astype(BF16)
    h_bwd[...] = dot(frm, to, NT).astype(BF16)
    flag[0] = (jnp.max(count) > 256.0).astype(I32)
    row = lax.broadcasted_iota(I32, (256, 128), 0)
    degree = jnp.zeros((256, 128), F32)
    for ref, n in ((own_to, 48), (halo_to, 8), (hub_to, 2)):
        for i in range(n):
            degree = degree + jnp.where(row == ref[i : i + 1, :], 1.0, 0.0)
    degree = jnp.sum(degree, axis=1, keepdims=True)
    inv[...] = jnp.broadcast_to(1.0 / (degree + 1.0), (256, 128))


def k_partial(flag, pos, l0, l1, l2, l3, far, features, incoming, fwd, *outs):
    hubs = incoming[:, 32:40, :].reshape(256, 128)
    x = jnp.concatenate([halves(features[...]), halves(hubs)], axis=0)
    for r in range(8):
        outs[r][...] = joined(dot(fwd[r], x))

    @pl.when(flag[0] != 0)
    def _():
        for r, block in enumerate(blocks_of((l0, l1, l2, l3, far))):
            outs[r][...] += joined(dot(rest(forward_count(*hots(pos, block))), x))


def k_halo(flag, halo_to, halo_from, incoming, h_fwd, own, out):
    x = halves(incoming[:, 0:32, :].reshape(1024, 128))
    out[...] = own[...] + joined(dot(h_fwd[...], x))

    @pl.when(flag[0] != 0)
    def _():
        to, frm = halo_hots(halo_to, halo_from)
        out[...] += joined(dot(rest(dot(to, frm, NT)), x))


def k_layer(a0, a1, a2, a3, a4, inv, features, w_neigh, w_root, bias, grad_out,
            output, grad_pre, grad_sum, mean):
    scale = inv[...]
    m = (a0[...] + a1[...] + a2[...] + a3[...] + a4[...]) * scale
    mean[...] = m
    pre = dot(m, w_neigh[...], NN, HIGH) + dot(features[...], w_root[...], NN, HIGH) + bias[...]
    negative = jnp.minimum(pre, 0.0)
    output[...] = jnp.where(pre > 0, pre, expm1(negative))
    g = grad_out[...] * jnp.where(pre > 0, 1.0, jnp.exp(negative))
    grad_pre[...] = g
    grad_sum[...] = dot(g, w_neigh[...], NT, HIGH) * scale


def k_weights(grad_pre, mean, features, out):
    g = grad_pre[...]
    out[0:16, 0:8, :] = dot(mean[...], g, TN, HIGH).reshape(16, 8, 128)
    out[16:32, 0:8, :] = dot(features[...], g, TN, HIGH).reshape(16, 8, 128)
    fill = jnp.broadcast_to(jnp.sum(g, axis=0, keepdims=True), (8, 128))
    for p in range(32):
        out[p, 8:16, :] = fill


def k_slots(flag, halo_to, halo_from, grad_sum, h_bwd, grad_pre, w_root, out, root):
    x = halves(grad_sum[...])
    out[...] = joined(dot(h_bwd[...], x))
    root[...] = dot(grad_pre[...], w_root[...], NT, HIGH)

    @pl.when(flag[0] != 0)
    def _():
        to, frm = halo_hots(halo_to, halo_from)
        out[...] += joined(dot(rest(dot(frm, to, NT)), x))


def k_back(flag, pos, l0, l1, l2, l3, far, g0, g1, g2, g3, g4, g5, g6, g7, bwd, root, local, hubs, total):
    xs = [halves(g[0:256, :]) for g in (g0, g1, g2, g3, g4, g5, g6, g7)]
    acc = dot(bwd[0], xs[0])
    for r in range(1, 8):
        acc = acc + dot(bwd[r], xs[r])
    total[...] = joined(acc)

    @pl.when(flag[0] != 0)
    def _():
        for r, block in enumerate(blocks_of((l0, l1, l2, l3, far))):
            total[...] += joined(dot(rest(backward_count(*hots(pos, block))), xs[r]))

    hubs[...] = total[256:512, :].reshape(32, 8, 128)
    local[...] = root[...] + total[0:256, :]


def k_sum(weights, out):
    out[...] = jnp.sum(weights[...], axis=0)


def k_pack(factor, hubs, near, far, out, bias):
    w = (near[...] + far[...]) * factor
    out[:, 0:8, :] = hubs[...]
    for p in range(32):
        out[p, 8:16, :] = w[0:8]
    bias[...] = w[8:9]


def k_scatter(returned, send, local, out):
    out[...] = local[...] + joined(dot(send_hot(send), halves(returned[...].reshape(1024, 128))))


def k_final(last, hub, local, out, w_neigh, w_root):
    rows = jnp.sum(last[:, 0:8, :], axis=0)
    out[...] = local[...]
    for j in range(8):
        out[pl.ds(hub[j], 1), :] += rows[j : j + 1, :]
    w_neigh[...] = last[0:16, 8:16, :].reshape(128, 128)
    w_root[...] = last[16:32, 8:16, :].reshape(128, 128)


def per_device(features, w_neigh, w_root, bias, grad_out, tile_coord, tile_edge,
               send_idx, halo_dst, halo_src, hub_idx, hub_dst, hub_src):
    send = send_idx.reshape(32, 32)
    hub = hub_idx.reshape(8)
    hub_to = hub_dst.reshape(2, 128)
    hub_from = hub_src.reshape(2, 128)
    halo_to = halo_dst.reshape(8, 128)
    halo_from = halo_src.reshape(8, 128)
    pos = lax.axis_index("blk").astype(I32).reshape(1)
    block = shape((256, 128))

    def swap(v):
        return lax.ppermute(v, "blk", [(i, i ^ 4) for i in range(8)])

    def turn(v, k):
        return lax.ppermute(v, "blk", [(i, i // 4 * 4 + (i % 4 + k) % 4) for i in range(8)])

    def exchange(v, axis):
        return lax.all_to_all(v, axis, split_axis=0, concat_axis=0, tiled=True)

    vm, sm, hb = (pl.BlockSpec(memory_space=s) for s in (pltpu.VMEM, pltpu.SMEM, pltpu.HBM))

    outgoing = call(
        k_send, shape((32, 40, 128)), (features, send, hub_idx.reshape(1, 8)), [hb] * 3,
        [pltpu.VMEM((256, 128), F32), pltpu.VMEM((32, 32), I32), pltpu.VMEM((1, 8), I32), pltpu.SemaphoreType.DMA((3,))],
        limit=60 << 20,
    )
    outgoing, coord = lax.optimization_barrier((outgoing, tile_coord.reshape(8, 2, 6)))
    incoming = exchange(outgoing, "grp")
    own_to, m0, m1, m2, m3 = call(
        k_lists, [shape((48, 128), I32)] + [shape((32, 128), I32)] * 4,
        (pos, coord, tile_edge.reshape(8, 6, 2, 128), hub_to, hub_from), [sm, sm, vm, vm, vm],
    )
    l3, l2, l1 = turn(m1, 1), turn(m2, 2), turn(m3, 3)
    far = swap(jnp.concatenate([m0[16:], l1[16:], l2[16:], l3[16:]], axis=0))
    lists = (pos, m0, l1, l2, l3, far)
    lm = [sm] + [vm] * 5
    h_fwd, h_bwd, inv, h_flag = call(
        k_boundary, (shape((256, 1024), BF16), shape((1024, 256), BF16), block, shape((1,), I32)),
        (own_to, halo_to, halo_from, hub_to), flops=1 << 31,
    )
    fwd, flag = call(k_fwd, (shape((8, 256, 512), BF16), shape((1,), I32)), lists, lm, flops=1 << 31)
    bwd = call(k_bwd, shape((8, 512, 256), BF16), lists, lm, flops=1 << 31)
    part = call(k_partial, [block] * 8, (flag, *lists, features, incoming, fwd), [sm, *lm, vm, vm, vm])
    other = part[4] + turn(part[5], 1) + turn(part[7], 3) + turn(part[6], 2)
    other, p1, p2, p3 = lax.optimization_barrier((other, part[1], part[2], part[3]))
    other = swap(other)
    near = [turn(p1, 1), turn(p3, 3), turn(p2, 2)]
    own = call(k_halo, block, (h_flag, halo_to, halo_from, incoming, h_fwd, part[0]), [sm] + [vm] * 5)
    inv, bwd = lax.optimization_barrier((inv, bwd))
    output, grad_pre, grad_sum, mean = call(
        k_layer, [block] * 4, (own, other, *near, inv, features, w_neigh, w_root, bias.reshape(1, 128), grad_out),
    )
    g4 = swap(grad_sum)
    g1, g3, g2 = turn(grad_sum, 3), turn(grad_sum, 1), turn(grad_sum, 2)
    weights = exchange(call(k_weights, shape((32, 16, 128)), (grad_pre, mean, features)), "grp")
    slots, root = call(
        k_slots, [shape((1024, 128)), block], (h_flag, halo_to, halo_from, grad_sum, h_bwd, grad_pre, w_root),
        [sm] + [vm] * 6,
    )
    g4, weights, g1, g2, g3, slots = lax.optimization_barrier((g4, weights, g1, g2, g3, slots))
    returned = exchange(slots.reshape(32, 32, 128), "grp")
    w = call(k_sum, shape((16, 128)), (weights,))
    w = w + turn(w, 1) + turn(w, 2) + turn(w, 3)
    w_far = swap(w)
    g5, g7, g6 = turn(g4, 3), turn(g4, 1), turn(g4, 2)
    local, hubs = call(
        k_back, [block, shape((32, 8, 128))],
        (flag, *lists, grad_sum, g1, g2, g3, g4, g5, g6, g7, bwd, root), [sm, *lm] + [vm] * 10,
        [pltpu.VMEM((512, 128), F32)],
    )
    factor = (256 * lax.axis_size("grp") * lax.axis_size("blk")) ** (-0.5)
    last, grad_bias = call(
        functools.partial(k_pack, factor), [shape((32, 16, 128)), shape((1, 128))], (hubs, w, w_far)
    )
    last = exchange(last, "grp")
    local = call(k_scatter, block, (returned, send, local))
    grad_features, grad_wn, grad_wr = call(
        k_final, [block, shape((128, 128)), shape((128, 128))], (last, hub, local), [vm, sm, vm]
    )
    return output, grad_features, grad_wn, grad_wr, grad_bias.reshape(128)


def solution(mesh):
    rows = P(("grp", "blk"), None)
    in_specs = (
        rows, P(), P(), P(), rows,
        P("grp", "blk", None, None, None),
        P("grp", "blk", None, None, None, None),
        P("grp", "blk", None, None),
        P("grp", "blk", None), P("grp", "blk", None), P("grp", "blk", None), P("grp", "blk", None), P("grp", "blk", None),
    )
    return jax.shard_map(
        per_device, mesh=mesh, in_specs=in_specs, out_specs=(rows, rows, P(), P(), P()), check_vma=False
    )
```

```python
import functools

import jax
import jax.numpy as jnp
from jax import lax
from jax.experimental import pallas as pl
from jax.experimental.pallas import tpu as pltpu
from jax.sharding import PartitionSpec as P

HIGH = lax.Precision.HIGHEST
F32, BF16, I32 = jnp.float32, jnp.bfloat16, jnp.int32
NT = (((1,), (1,)), ((), ()))
NN = (((1,), (0,)), ((), ()))
TN = (((0,), (0,)), ((), ()))


def dot(a, b, dims=NN, precision=None):
    return lax.dot_general(a, b, dims, precision=precision, preferred_element_type=F32)


def halves(x):
    high = x.astype(BF16)
    low = (x - high.astype(F32)).astype(BF16)
    return jnp.concatenate([high, low], axis=1)


def joined(y):
    n = y.shape[1] // 2
    return y[:, :n] + y[:, n:]


def one_hot(idx, rows):
    n = idx.shape[1]
    row = lax.broadcasted_iota(I32, (rows, n), 0)
    return jnp.where(row == idx, 1.0, 0.0).astype(BF16)


def lanes(ref_rows):
    return jnp.concatenate(ref_rows, axis=1)


def call(kernel, out_shape, args, specs=None, scratch=(), flops=1 << 28, limit=16 << 20):
    whole = pl.BlockSpec(memory_space=pltpu.VMEM)
    size = sum(int(a.size) * a.dtype.itemsize for a in args)
    return pl.pallas_call(
        kernel,
        out_shape=out_shape,
        in_specs=[whole] * len(args) if specs is None else specs,
        out_specs=jax.tree.map(
            lambda s: pl.BlockSpec(memory_space=pltpu.SMEM if s.shape == (1,) else pltpu.VMEM), out_shape
        ),
        scratch_shapes=list(scratch),
        compiler_params=pltpu.CompilerParams(vmem_limit_bytes=limit),
        cost_estimate=pl.CostEstimate(flops=flops, bytes_accessed=size, transcendentals=0),
    )(*args)


def shape(s, d=F32):
    return jax.ShapeDtypeStruct(s, d)


def expm1(x):
    series = x * (1 + x * (1 / 2) * (1 + x * (1 / 3) * (1 + x * (1 / 4) * (1 + x * (1 / 5) * (1 + x * (1 / 6) * (1 + x * (1 / 7)))))))
    return jnp.where(x > -0.35, series, jnp.exp(x) - 1.0)


def send_hot(send):
    return lanes([one_hot(lanes([send[4 * i + j : 4 * i + j + 1, :] for j in range(4)]), 256) for i in range(8)])


def k_send(features_hbm, send_hbm, hub_hbm, out, features, send, hub, sems):
    pairs = ((features_hbm, features), (send_hbm, send), (hub_hbm, hub))
    copies = [pltpu.make_async_copy(src, dst, sems.at[n]) for n, (src, dst) in enumerate(pairs)]
    for copy in copies:
        copy.start()
    for copy in copies:
        copy.wait()
    x = halves(features[...])
    out[:, 0:32, :] = joined(dot(send_hot(send), x, TN)).reshape(32, 32, 128)
    hub_rows = joined(dot(one_hot(hub[...], 256), x, TN))
    for p in range(32):
        out[p, 32:40, :] = hub_rows


def k_lists(pos, coord, edge, hub_to, hub_from, own_to, *outs):
    me = pos[0]
    for b in range(8):
        for t in range(6):
            own_to[b * 6 + t : b * 6 + t + 1, :] = edge[b, t, 0:1, :] + coord[b, 0, t] * 128
    for d in range(2):
        for k in range(4):
            b = jnp.bitwise_xor(me // 4, d) * 4 + (me % 4 + k) % 4
            at = d * 16
            for t in range(6):
                outs[k][at + t : at + t + 1, :] = edge[b, t, 0:1, :] + coord[b, 0, t] * 128
                outs[k][at + 6 + t : at + 7 + t, :] = edge[b, t, 1:2, :] + coord[b, 1, t] * 128
            outs[k][at + 12 : at + 14, :] = hub_to[...]
            outs[k][at + 14 : at + 16, :] = hub_from[...]


def hots(pos, block):
    me = pos[0]
    to = lanes([one_hot(block[i : i + 1, :], 256) for i in range(6)])
    frm = lanes([one_hot(block[i : i + 1, :], 256) for i in range(6, 12)])
    h_to = lanes([one_hot(block[i : i + 1, :], 256) for i in range(12, 14)])
    codes = [block[i : i + 1, :] for i in range(14, 16)]
    rows = [jnp.where((c >> 3) % 8 == me, (c >> 6) * 8 + c % 8, -1) for c in codes]
    return to, frm, h_to, lanes([one_hot(c, 256) for c in rows])


def blocks_of(lists):
    own, l1, l2, l3, far = lists
    return [ref[0:16, :] for ref in (own, l1, l2, l3)] + [far[16 * k : 16 * k + 16, :] for k in range(4)]


def halo_hots(halo_to, halo_from):
    to = lanes([one_hot(halo_to[i : i + 1, :], 256) for i in range(8)])
    return to, lanes([one_hot(halo_from[i : i + 1, :], 1024) for i in range(8)])


def rest(count):
    return (count - count.astype(BF16).astype(F32)).astype(BF16)


def forward_count(to, frm, h_to, h_frm):
    return jnp.concatenate([dot(to, frm, NT), dot(h_to, h_frm, NT)], axis=1)


def backward_count(to, frm, h_to, h_frm):
    return jnp.concatenate([dot(frm, to, NT), dot(h_frm, h_to, NT)], axis=0)


def k_fwd(pos, *rest_refs):
    *lists, fwd, flag = rest_refs
    blocks = [ref[0:16, :] for ref in lists] if len(lists) == 4 else [lists[0][16 * k : 16 * k + 16, :] for k in range(4)]
    top = jnp.float32(0.0)
    for r, block in enumerate(blocks):
        count = forward_count(*hots(pos, block))
        top = jnp.maximum(top, jnp.max(count))
        fwd[r] = count.astype(BF16)
    flag[0] = (top > 256.0).astype(I32)


def k_bwd(pos, l0, l1, l2, l3, far, bwd):
    for r, block in enumerate(blocks_of((l0, l1, l2, l3, far))):
        bwd[r] = backward_count(*hots(pos, block)).astype(BF16)


def k_boundary(own_to, halo_to, halo_from, hub_to, h_fwd, h_bwd, inv, flag):
    to, frm = halo_hots(halo_to, halo_from)
    count = dot(to, frm, NT)
    h_fwd[...] = count.astype(BF16)
    h_bwd[...] = dot(frm, to, NT).astype(BF16)
    flag[0] = (jnp.max(count) > 256.0).astype(I32)
    row = lax.broadcasted_iota(I32, (256, 128), 0)
    degree = jnp.zeros((256, 128), F32)
    for ref, n in ((own_to, 48), (halo_to, 8), (hub_to, 2)):
        for i in range(n):
            degree = degree + jnp.where(row == ref[i : i + 1, :], 1.0, 0.0)
    degree = jnp.sum(degree, axis=1, keepdims=True)
    inv[...] = jnp.broadcast_to(1.0 / (degree + 1.0), (256, 128))


def k_partial(flag, pos, *rest_refs):
    *lists, features, incoming, fwd, o0, o1, o2, o3 = rest_refs
    outs = (o0, o1, o2, o3)
    hubs = incoming[:, 32:40, :].reshape(256, 128)
    x = jnp.concatenate([halves(features[...]), halves(hubs)], axis=0)
    for r in range(4):
        outs[r][...] = joined(dot(fwd[r], x))

    @pl.when(flag[0] != 0)
    def _():
        blocks = [ref[0:16, :] for ref in lists] if len(lists) == 4 else [lists[0][16 * k : 16 * k + 16, :] for k in range(4)]
        for r, block in enumerate(blocks):
            outs[r][...] += joined(dot(rest(forward_count(*hots(pos, block))), x))


def k_halo(flag, halo_to, halo_from, incoming, h_fwd, own, out):
    x = halves(incoming[:, 0:32, :].reshape(1024, 128))
    out[...] = own[...] + joined(dot(h_fwd[...], x))

    @pl.when(flag[0] != 0)
    def _():
        to, frm = halo_hots(halo_to, halo_from)
        out[...] += joined(dot(rest(dot(to, frm, NT)), x))


def k_layer(a0, a1, a2, a3, a4, inv, features, w_neigh, w_root, bias, grad_out,
            output, grad_pre, grad_sum, mean):
    scale = inv[...]
    m = (a0[...] + a1[...] + a2[...] + a3[...] + a4[...]) * scale
    mean[...] = m
    pre = dot(m, w_neigh[...], NN, HIGH) + dot(features[...], w_root[...], NN, HIGH) + bias[...]
    negative = jnp.minimum(pre, 0.0)
    output[...] = jnp.where(pre > 0, pre, expm1(negative))
    g = grad_out[...] * jnp.where(pre > 0, 1.0, jnp.exp(negative))
    grad_pre[...] = g
    grad_sum[...] = dot(g, w_neigh[...], NT, HIGH) * scale


def k_weights(grad_pre, mean, features, out):
    g = grad_pre[...]
    out[0:16, 0:8, :] = dot(mean[...], g, TN, HIGH).reshape(16, 8, 128)
    out[16:32, 0:8, :] = dot(features[...], g, TN, HIGH).reshape(16, 8, 128)
    fill = jnp.broadcast_to(jnp.sum(g, axis=0, keepdims=True), (8, 128))
    for p in range(32):
        out[p, 8:16, :] = fill


def k_slots(flag, halo_to, halo_from, grad_sum, h_bwd, out):
    x = halves(grad_sum[...])
    out[...] = joined(dot(h_bwd[...], x))

    @pl.when(flag[0] != 0)
    def _():
        to, frm = halo_hots(halo_to, halo_from)
        out[...] += joined(dot(rest(dot(frm, to, NT)), x))


def k_back(flag, flag_far, pos, l0, l1, l2, l3, far, g0, g1, g2, g3, g4, g5, g6, g7, bwd, local, hubs, total):
    xs = [halves(g[0:256, :]) for g in (g0, g1, g2, g3, g4, g5, g6, g7)]
    acc = dot(bwd[0], xs[0])
    for r in range(1, 8):
        acc = acc + dot(bwd[r], xs[r])
    total[...] = joined(acc)

    @pl.when(flag[0] + flag_far[0] != 0)
    def _():
        for r, block in enumerate(blocks_of((l0, l1, l2, l3, far))):
            total[...] += joined(dot(rest(backward_count(*hots(pos, block))), xs[r]))

    hubs[...] = total[256:512, :].reshape(32, 8, 128)
    local[...] = total[0:256, :]


def k_sum(weights, out):
    out[...] = jnp.sum(weights[...], axis=0)


def k_pack(factor, hubs, near, far, out, bias):
    w = (near[...] + far[...]) * factor
    out[:, 0:8, :] = hubs[...]
    for p in range(32):
        out[p, 8:16, :] = w[0:8]
    bias[...] = w[8:9]


def k_scatter(returned, send, local, grad_pre, w_root, out):
    root = dot(grad_pre[...], w_root[...], NT, HIGH)
    out[...] = local[...] + root + joined(dot(send_hot(send), halves(returned[...].reshape(1024, 128))))


def k_final(last, hub, local, out, w_neigh, w_root):
    rows = jnp.sum(last[:, 0:8, :], axis=0)
    out[...] = local[...]
    for j in range(8):
        out[pl.ds(hub[j], 1), :] += rows[j : j + 1, :]
    w_neigh[...] = last[0:16, 8:16, :].reshape(128, 128)
    w_root[...] = last[16:32, 8:16, :].reshape(128, 128)


def per_device(features, w_neigh, w_root, bias, grad_out, tile_coord, tile_edge,
               send_idx, halo_dst, halo_src, hub_idx, hub_dst, hub_src):
    send = send_idx.reshape(32, 32)
    hub = hub_idx.reshape(8)
    hub_to = hub_dst.reshape(2, 128)
    hub_from = hub_src.reshape(2, 128)
    halo_to = halo_dst.reshape(8, 128)
    halo_from = halo_src.reshape(8, 128)
    pos = lax.axis_index("blk").astype(I32).reshape(1)
    block = shape((256, 128))

    def swap(v):
        return lax.ppermute(v, "blk", [(i, i ^ 4) for i in range(8)])

    def turn(v, k):
        return lax.ppermute(v, "blk", [(i, i // 4 * 4 + (i % 4 + k) % 4) for i in range(8)])

    def exchange(v, axis):
        return lax.all_to_all(v, axis, split_axis=0, concat_axis=0, tiled=True)

    vm, sm, hb = (pl.BlockSpec(memory_space=s) for s in (pltpu.VMEM, pltpu.SMEM, pltpu.HBM))

    outgoing = call(
        k_send, shape((32, 40, 128)), (features, send, hub_idx.reshape(1, 8)), [hb] * 3,
        [pltpu.VMEM((256, 128), F32), pltpu.VMEM((32, 32), I32), pltpu.VMEM((1, 8), I32), pltpu.SemaphoreType.DMA((3,))],
        limit=60 << 20,
    )
    outgoing, coord = lax.optimization_barrier((outgoing, tile_coord.reshape(8, 2, 6)))
    incoming = exchange(outgoing, "grp")
    own_to, m0, m1, m2, m3 = call(
        k_lists, [shape((48, 128), I32)] + [shape((32, 128), I32)] * 4,
        (pos, coord, tile_edge.reshape(8, 6, 2, 128), hub_to, hub_from), [sm, sm, vm, vm, vm],
    )
    l3, l2, l1 = turn(m1, 1), turn(m2, 2), turn(m3, 3)
    far = swap(jnp.concatenate([m0[16:], l1[16:], l2[16:], l3[16:]], axis=0))
    lists = (pos, m0, l1, l2, l3, far)
    lm = [sm] + [vm] * 5
    h_fwd, h_bwd, inv, h_flag = call(
        k_boundary, (shape((256, 1024), BF16), shape((1024, 256), BF16), block, shape((1,), I32)),
        (own_to, halo_to, halo_from, hub_to), flops=1 << 31,
    )
    counts = (shape((4, 256, 512), BF16), shape((1,), I32))
    fwd_near, flag_near = call(k_fwd, counts, lists[:5], lm[:5], flops=1 << 30)
    fwd_far, flag_far = call(k_fwd, counts, (pos, far), lm[:2], flops=1 << 30)
    bwd = call(k_bwd, shape((8, 512, 256), BF16), lists, lm, flops=1 << 31)
    part = call(k_partial, [block] * 4, (flag_far, pos, far, features, incoming, fwd_far), [sm, sm] + [vm] * 4)
    o1, o3, o2 = turn(part[1], 1), turn(part[3], 3), turn(part[2], 2)
    own_part = call(
        k_partial, [block] * 4, (flag_near, *lists[:5], features, incoming, fwd_near), [sm, *lm[:5]] + [vm] * 3
    )
    other = part[0] + o1 + o3 + o2
    part = own_part
    other, p1, p2, p3 = lax.optimization_barrier((other, part[1], part[2], part[3]))
    other = swap(other)
    own = call(k_halo, block, (h_flag, halo_to, halo_from, incoming, h_fwd, part[0]), [sm] + [vm] * 5)
    own, p2 = lax.optimization_barrier((own, p2))
    near = [turn(p1, 1), turn(p3, 3), turn(p2, 2)]
    output, grad_pre, grad_sum, mean = call(
        k_layer, [block] * 4, (own, other, *near, inv, features, w_neigh, w_root, bias.reshape(1, 128), grad_out),
    )
    g4 = swap(grad_sum)
    g1, g3, g2 = turn(grad_sum, 3), turn(grad_sum, 1), turn(grad_sum, 2)
    weights = exchange(call(k_weights, shape((32, 16, 128)), (grad_pre, mean, features)), "grp")
    slots = call(k_slots, shape((1024, 128)), (h_flag, halo_to, halo_from, grad_sum, h_bwd), [sm] + [vm] * 4)
    weights, g1, g2, g3, g4, slots, bwd = lax.optimization_barrier((weights, g1, g2, g3, g4, slots, bwd))
    returned = exchange(slots.reshape(32, 32, 128), "grp")
    w = call(k_sum, shape((16, 128)), (weights,))
    w = w + turn(w, 1) + turn(w, 2) + turn(w, 3)
    w_far = swap(w)
    g5, g7, g6 = turn(g4, 3), turn(g4, 1), turn(g4, 2)
    local, hubs = call(
        k_back, [block, shape((32, 8, 128))],
        (flag_near, flag_far, *lists, grad_sum, g1, g2, g3, g4, g5, g6, g7, bwd), [sm, sm, *lm] + [vm] * 9,
        [pltpu.VMEM((512, 128), F32)],
    )
    factor = (256 * lax.axis_size("grp") * lax.axis_size("blk")) ** (-0.5)
    last, grad_bias = call(
        functools.partial(k_pack, factor), [shape((32, 16, 128)), shape((1, 128))], (hubs, w, w_far)
    )
    last = exchange(last, "grp")
    local = call(k_scatter, block, (returned, send, local, grad_pre, w_root))
    grad_features, grad_wn, grad_wr = call(
        k_final, [block, shape((128, 128)), shape((128, 128))], (last, hub, local), [vm, sm, vm]
    )
    return output, grad_features, grad_wn, grad_wr, grad_bias.reshape(128)


def solution(mesh):
    rows = P(("grp", "blk"), None)
    in_specs = (
        rows, P(), P(), P(), rows,
        P("grp", "blk", None, None, None),
        P("grp", "blk", None, None, None, None),
        P("grp", "blk", None, None),
        P("grp", "blk", None), P("grp", "blk", None), P("grp", "blk", None), P("grp", "blk", None), P("grp", "blk", None),
    )
    return jax.shard_map(
        per_device, mesh=mesh, in_specs=in_specs, out_specs=(rows, rows, P(), P(), P()), check_vma=False
    )
```

```python
import functools

import jax
import jax.numpy as jnp
from jax import lax
from jax.experimental import pallas as pl
from jax.experimental.pallas import tpu as pltpu
from jax.sharding import PartitionSpec as P

HIGH = lax.Precision.HIGHEST
F32, BF16, I32 = jnp.float32, jnp.bfloat16, jnp.int32
NT = (((1,), (1,)), ((), ()))
NN = (((1,), (0,)), ((), ()))
TN = (((0,), (0,)), ((), ()))


def dot(a, b, dims=NN, precision=None):
    return lax.dot_general(a, b, dims, precision=precision, preferred_element_type=F32)


def halves(x):
    high = x.astype(BF16)
    low = (x - high.astype(F32)).astype(BF16)
    return jnp.concatenate([high, low], axis=1)


def joined(y):
    n = y.shape[1] // 2
    return y[:, :n] + y[:, n:]


def one_hot(idx, rows):
    n = idx.shape[1]
    row = lax.broadcasted_iota(I32, (rows, n), 0)
    return jnp.where(row == idx, 1.0, 0.0).astype(BF16)


def lanes(ref_rows):
    return jnp.concatenate(ref_rows, axis=1)


def call(kernel, out_shape, args, specs=None, scratch=(), flops=1 << 28, limit=16 << 20):
    whole = pl.BlockSpec(memory_space=pltpu.VMEM)
    size = sum(int(a.size) * a.dtype.itemsize for a in args)
    return pl.pallas_call(
        kernel,
        out_shape=out_shape,
        in_specs=[whole] * len(args) if specs is None else specs,
        out_specs=jax.tree.map(
            lambda s: pl.BlockSpec(memory_space=pltpu.SMEM if s.shape == (1,) else pltpu.VMEM), out_shape
        ),
        scratch_shapes=list(scratch),
        compiler_params=pltpu.CompilerParams(vmem_limit_bytes=limit),
        cost_estimate=pl.CostEstimate(flops=flops, bytes_accessed=size, transcendentals=0),
    )(*args)


def shape(s, d=F32):
    return jax.ShapeDtypeStruct(s, d)


def expm1(x):
    series = x * (1 + x * (1 / 2) * (1 + x * (1 / 3) * (1 + x * (1 / 4) * (1 + x * (1 / 5) * (1 + x * (1 / 6) * (1 + x * (1 / 7)))))))
    return jnp.where(x > -0.35, series, jnp.exp(x) - 1.0)


def send_hot(send):
    return lanes([one_hot(lanes([send[4 * i + j : 4 * i + j + 1, :] for j in range(4)]), 256) for i in range(8)])


def k_send(features_hbm, send_hbm, hub_hbm, out, features, send, hub, sems):
    pairs = ((features_hbm, features), (send_hbm, send), (hub_hbm, hub))
    copies = [pltpu.make_async_copy(src, dst, sems.at[n]) for n, (src, dst) in enumerate(pairs)]
    for copy in copies:
        copy.start()
    for copy in copies:
        copy.wait()
    x = halves(features[...])
    out[:, 0:32, :] = joined(dot(send_hot(send), x, TN)).reshape(32, 32, 128)
    hub_rows = joined(dot(one_hot(hub[...], 256), x, TN))
    for p in range(32):
        out[p, 32:40, :] = hub_rows


def k_lists(pos, coord, edge, hub_to, hub_from, own_to, *outs):
    me = pos[0]
    for b in range(8):
        for t in range(6):
            own_to[b * 6 + t : b * 6 + t + 1, :] = edge[b, t, 0:1, :] + coord[b, 0, t] * 128
    for d in range(2):
        for k in range(4):
            b = jnp.bitwise_xor(me // 4, d) * 4 + (me % 4 + k) % 4
            at = d * 16
            for t in range(6):
                outs[k][at + t : at + t + 1, :] = edge[b, t, 0:1, :] + coord[b, 0, t] * 128
                outs[k][at + 6 + t : at + 7 + t, :] = edge[b, t, 1:2, :] + coord[b, 1, t] * 128
            outs[k][at + 12 : at + 14, :] = hub_to[...]
            outs[k][at + 14 : at + 16, :] = hub_from[...]


def hots(pos, block):
    me = pos[0]
    to = lanes([one_hot(block[i : i + 1, :], 256) for i in range(6)])
    frm = lanes([one_hot(block[i : i + 1, :], 256) for i in range(6, 12)])
    h_to = lanes([one_hot(block[i : i + 1, :], 256) for i in range(12, 14)])
    codes = [block[i : i + 1, :] for i in range(14, 16)]
    rows = [jnp.where((c >> 3) % 8 == me, (c >> 6) * 8 + c % 8, -1) for c in codes]
    return to, frm, h_to, lanes([one_hot(c, 256) for c in rows])


def blocks_of(lists):
    own, l1, l2, l3, far = lists
    return [ref[0:16, :] for ref in (own, l1, l2, l3)] + [far[16 * k : 16 * k + 16, :] for k in range(4)]


def halo_hots(halo_to, halo_from):
    to = lanes([one_hot(halo_to[i : i + 1, :], 256) for i in range(8)])
    return to, lanes([one_hot(halo_from[i : i + 1, :], 1024) for i in range(8)])


def rest(count):
    return (count - count.astype(BF16).astype(F32)).astype(BF16)


def forward_count(to, frm, h_to, h_frm):
    return jnp.concatenate([dot(to, frm, NT), dot(h_to, h_frm, NT)], axis=1)


def backward_count(to, frm, h_to, h_frm):
    return jnp.concatenate([dot(frm, to, NT), dot(h_frm, h_to, NT)], axis=0)


def k_fwd(pos, l0, l1, l2, l3, far, fwd, flag):
    top = jnp.float32(0.0)
    for r, block in enumerate(blocks_of((l0, l1, l2, l3, far))):
        count = forward_count(*hots(pos, block))
        top = jnp.maximum(top, jnp.max(count))
        fwd[r] = count.astype(BF16)
    flag[0] = (top > 256.0).astype(I32)


def k_bwd(pos, l0, l1, l2, l3, far, bwd):
    for r, block in enumerate(blocks_of((l0, l1, l2, l3, far))):
        bwd[r] = backward_count(*hots(pos, block)).astype(BF16)


def k_boundary(own_to, halo_to, halo_from, hub_to, h_fwd, h_bwd, inv, flag):
    to, frm = halo_hots(halo_to, halo_from)
    count = dot(to, frm, NT)
    h_fwd[...] = count.astype(BF16)
    h_bwd[...] = dot(frm, to, NT).astype(BF16)
    flag[0] = (jnp.max(count) > 256.0).astype(I32)
    row = lax.broadcasted_iota(I32, (256, 128), 0)
    degree = jnp.zeros((256, 128), F32)
    for ref, n in ((own_to, 48), (halo_to, 8), (hub_to, 2)):
        for i in range(n):
            degree = degree + jnp.where(row == ref[i : i + 1, :], 1.0, 0.0)
    degree = jnp.sum(degree, axis=1, keepdims=True)
    inv[...] = jnp.broadcast_to(1.0 / (degree + 1.0), (256, 128))


def k_partial(flag, pos, l0, l1, l2, l3, far, features, incoming, fwd, *outs):
    hubs = incoming[:, 32:40, :].reshape(256, 128)
    x = jnp.concatenate([halves(features[...]), halves(hubs)], axis=0)
    for r in range(8):
        outs[r][...] = joined(dot(fwd[r], x))

    @pl.when(flag[0] != 0)
    def _():
        for r, block in enumerate(blocks_of((l0, l1, l2, l3, far))):
            outs[r][...] += joined(dot(rest(forward_count(*hots(pos, block))), x))


def k_halo(flag, halo_to, halo_from, incoming, h_fwd, own, out):
    x = halves(incoming[:, 0:32, :].reshape(1024, 128))
    out[...] = own[...] + joined(dot(h_fwd[...], x))

    @pl.when(flag[0] != 0)
    def _():
        to, frm = halo_hots(halo_to, halo_from)
        out[...] += joined(dot(rest(dot(to, frm, NT)), x))


def k_layer(a0, a1, a2, a3, a4, inv, features, w_neigh, w_root, bias, grad_out,
            output, grad_pre, grad_sum, mean):
    scale = inv[...]
    m = (a0[...] + a1[...] + a2[...] + a3[...] + a4[...]) * scale
    mean[...] = m
    pre = dot(m, w_neigh[...], NN, HIGH) + dot(features[...], w_root[...], NN, HIGH) + bias[...]
    negative = jnp.minimum(pre, 0.0)
    output[...] = jnp.where(pre > 0, pre, expm1(negative))
    g = grad_out[...] * jnp.where(pre > 0, 1.0, jnp.exp(negative))
    grad_pre[...] = g
    grad_sum[...] = dot(g, w_neigh[...], NT, HIGH) * scale


def k_weights(grad_pre, mean, features, out):
    g = grad_pre[...]
    out[0:16, 0:8, :] = dot(mean[...], g, TN, HIGH).reshape(16, 8, 128)
    out[16:32, 0:8, :] = dot(features[...], g, TN, HIGH).reshape(16, 8, 128)
    fill = jnp.broadcast_to(jnp.sum(g, axis=0, keepdims=True), (8, 128))
    for p in range(32):
        out[p, 8:16, :] = fill


def k_slots(flag, halo_to, halo_from, grad_sum, h_bwd, out):
    x = halves(grad_sum[...])
    out[...] = joined(dot(h_bwd[...], x))

    @pl.when(flag[0] != 0)
    def _():
        to, frm = halo_hots(halo_to, halo_from)
        out[...] += joined(dot(rest(dot(frm, to, NT)), x))


def back_sum(low, blocks, pos, grads, bwd, at, total):
    xs = [halves(g[...]) for g in grads]
    acc = dot(bwd[at], xs[0])
    for r in range(1, 4):
        acc = acc + dot(bwd[at + r], xs[r])
    total[...] += joined(acc)

    @pl.when(low)
    def _():
        for r, block in enumerate(blocks()):
            total[...] += joined(dot(rest(backward_count(*hots(pos, block))), xs[r]))


def k_back_near(flag, pos, l0, l1, l2, l3, g0, g1, g2, g3, bwd, total):
    total[...] = jnp.zeros_like(total)
    back_sum(flag[0] != 0, lambda: [ref[0:16, :] for ref in (l0, l1, l2, l3)], pos, (g0, g1, g2, g3), bwd, 0, total)


def k_back(flag, pos, far, g4, g5, g6, g7, bwd, near, local, hubs, total):
    total[...] = near[...]
    blocks = lambda: [far[16 * k : 16 * k + 16, :] for k in range(4)]
    back_sum(flag[0] != 0, blocks, pos, (g4, g5, g6, g7), bwd, 4, total)
    hubs[...] = total[256:512, :].reshape(32, 8, 128)
    local[...] = total[0:256, :]


def k_sum(weights, out):
    out[...] = jnp.sum(weights[...], axis=0)


def k_pack(factor, hubs, near, far, out, bias):
    w = (near[...] + far[...]) * factor
    out[:, 0:8, :] = hubs[...]
    for p in range(32):
        out[p, 8:16, :] = w[0:8]
    bias[...] = w[8:9]


def k_scatter(returned, send, local, grad_pre, w_root, out):
    root = dot(grad_pre[...], w_root[...], NT, HIGH)
    out[...] = local[...] + root + joined(dot(send_hot(send), halves(returned[...].reshape(1024, 128))))


def k_final(last, hub, local, out, w_neigh, w_root):
    rows = jnp.sum(last[:, 0:8, :], axis=0)
    out[...] = local[...]
    for j in range(8):
        out[pl.ds(hub[j], 1), :] += rows[j : j + 1, :]
    w_neigh[...] = last[0:16, 8:16, :].reshape(128, 128)
    w_root[...] = last[16:32, 8:16, :].reshape(128, 128)


def per_device(features, w_neigh, w_root, bias, grad_out, tile_coord, tile_edge,
               send_idx, halo_dst, halo_src, hub_idx, hub_dst, hub_src):
    send = send_idx.reshape(32, 32)
    hub = hub_idx.reshape(8)
    hub_to = hub_dst.reshape(2, 128)
    hub_from = hub_src.reshape(2, 128)
    halo_to = halo_dst.reshape(8, 128)
    halo_from = halo_src.reshape(8, 128)
    pos = lax.axis_index("blk").astype(I32).reshape(1)
    block = shape((256, 128))

    def swap(v):
        return lax.ppermute(v, "blk", [(i, i ^ 4) for i in range(8)])

    def turn(v, k):
        return lax.ppermute(v, "blk", [(i, i // 4 * 4 + (i % 4 + k) % 4) for i in range(8)])

    def exchange(v, axis):
        return lax.all_to_all(v, axis, split_axis=0, concat_axis=0, tiled=True)

    vm, sm, hb = (pl.BlockSpec(memory_space=s) for s in (pltpu.VMEM, pltpu.SMEM, pltpu.HBM))

    outgoing = call(
        k_send, shape((32, 40, 128)), (features, send, hub_idx.reshape(1, 8)), [hb] * 3,
        [pltpu.VMEM((256, 128), F32), pltpu.VMEM((32, 32), I32), pltpu.VMEM((1, 8), I32), pltpu.SemaphoreType.DMA((3,))],
        limit=60 << 20,
    )
    outgoing, coord = lax.optimization_barrier((outgoing, tile_coord.reshape(8, 2, 6)))
    incoming = exchange(outgoing, "grp")
    own_to, m0, m1, m2, m3 = call(
        k_lists, [shape((48, 128), I32)] + [shape((32, 128), I32)] * 4,
        (pos, coord, tile_edge.reshape(8, 6, 2, 128), hub_to, hub_from), [sm, sm, vm, vm, vm],
    )
    l3, l2, l1 = turn(m1, 1), turn(m2, 2), turn(m3, 3)
    far = swap(jnp.concatenate([m0[16:], l1[16:], l2[16:], l3[16:]], axis=0))
    lists = (pos, m0, l1, l2, l3, far)
    lm = [sm] + [vm] * 5
    h_fwd, h_bwd, inv, h_flag = call(
        k_boundary, (shape((256, 1024), BF16), shape((1024, 256), BF16), block, shape((1,), I32)),
        (own_to, halo_to, halo_from, hub_to), flops=1 << 31,
    )
    fwd, flag = call(k_fwd, (shape((8, 256, 512), BF16), shape((1,), I32)), lists, lm, flops=1 << 31)
    bwd = call(k_bwd, shape((8, 512, 256), BF16), lists, lm, flops=1 << 31)
    part = call(k_partial, [block] * 8, (flag, *lists, features, incoming, fwd), [sm, *lm, vm, vm, vm])
    other = part[4] + turn(part[5], 1) + turn(part[7], 3) + turn(part[6], 2)
    other, p1, p2, p3 = lax.optimization_barrier((other, part[1], part[2], part[3]))
    other = swap(other)
    near = [turn(p2, 2), turn(p1, 1), turn(p3, 3)]
    own = call(k_halo, block, (h_flag, halo_to, halo_from, incoming, h_fwd, part[0]), [sm] + [vm] * 5)
    inv, bwd = lax.optimization_barrier((inv, bwd))
    output, grad_pre, grad_sum, mean = call(
        k_layer, [block] * 4, (own, other, *near, inv, features, w_neigh, w_root, bias.reshape(1, 128), grad_out),
    )
    g4 = swap(grad_sum)
    g1, g3, g2 = turn(grad_sum, 3), turn(grad_sum, 1), turn(grad_sum, 2)
    weights = exchange(call(k_weights, shape((32, 16, 128)), (grad_pre, mean, features)), "grp")
    slots = call(k_slots, shape((1024, 128)), (h_flag, halo_to, halo_from, grad_sum, h_bwd), [sm] + [vm] * 4)
    g4, g1, g2, g3 = lax.optimization_barrier((g4, g1, g2, g3))
    back = call(
        k_back_near, shape((512, 128)), (flag, *lists[:5], grad_sum, g1, g2, g3, bwd), [sm, *lm[:5]] + [vm] * 5
    )
    weights, back, slots = lax.optimization_barrier((weights, back, slots))
    w = call(k_sum, shape((16, 128)), (weights,))
    w, slots = lax.optimization_barrier((w, slots))
    returned = exchange(slots.reshape(32, 32, 128), "grp")
    w = w + turn(w, 1) + turn(w, 2) + turn(w, 3)
    w_far = swap(w)
    g5, g7, g6 = turn(g4, 3), turn(g4, 1), turn(g4, 2)
    local, hubs = call(
        k_back, [block, shape((32, 8, 128))],
        (flag, pos, far, g4, g5, g6, g7, bwd, back), [sm, sm] + [vm] * 7,
        [pltpu.VMEM((512, 128), F32)],
    )
    factor = (256 * lax.axis_size("grp") * lax.axis_size("blk")) ** (-0.5)
    last, grad_bias = call(
        functools.partial(k_pack, factor), [shape((32, 16, 128)), shape((1, 128))], (hubs, w, w_far)
    )
    last = exchange(last, "grp")
    local = call(k_scatter, block, (returned, send, local, grad_pre, w_root))
    grad_features, grad_wn, grad_wr = call(
        k_final, [block, shape((128, 128)), shape((128, 128))], (last, hub, local), [vm, sm, vm]
    )
    return output, grad_features, grad_wn, grad_wr, grad_bias.reshape(128)


def solution(mesh):
    rows = P(("grp", "blk"), None)
    in_specs = (
        rows, P(), P(), P(), rows,
        P("grp", "blk", None, None, None),
        P("grp", "blk", None, None, None, None),
        P("grp", "blk", None, None),
        P("grp", "blk", None), P("grp", "blk", None), P("grp", "blk", None), P("grp", "blk", None), P("grp", "blk", None),
    )
    return jax.shard_map(
        per_device, mesh=mesh, in_specs=in_specs, out_specs=(rows, rows, P(), P(), P()), check_vma=False
    )
```

```python
import functools

import jax
import jax.numpy as jnp
from jax import lax
from jax.experimental import pallas as pl
from jax.experimental.pallas import tpu as pltpu
from jax.sharding import PartitionSpec as P

HIGH = lax.Precision.HIGHEST
F32, BF16, I32 = jnp.float32, jnp.bfloat16, jnp.int32
NT = (((1,), (1,)), ((), ()))
NN = (((1,), (0,)), ((), ()))
TN = (((0,), (0,)), ((), ()))


def dot(a, b, dims=NN, precision=None):
    return lax.dot_general(a, b, dims, precision=precision, preferred_element_type=F32)


def halves(x):
    high = x.astype(BF16)
    low = (x - high.astype(F32)).astype(BF16)
    return jnp.concatenate([high, low], axis=1)


def joined(y):
    n = y.shape[1] // 2
    return y[:, :n] + y[:, n:]


def one_hot(idx, rows):
    n = idx.shape[1]
    row = lax.broadcasted_iota(I32, (rows, n), 0)
    return jnp.where(row == idx, 1.0, 0.0).astype(BF16)


def lanes(ref_rows):
    return jnp.concatenate(ref_rows, axis=1)


def call(kernel, out_shape, args, specs=None, scratch=(), flops=1 << 28, limit=16 << 20):
    whole = pl.BlockSpec(memory_space=pltpu.VMEM)
    size = sum(int(a.size) * a.dtype.itemsize for a in args)
    return pl.pallas_call(
        kernel,
        out_shape=out_shape,
        in_specs=[whole] * len(args) if specs is None else specs,
        out_specs=jax.tree.map(
            lambda s: pl.BlockSpec(memory_space=pltpu.SMEM if s.shape == (1,) else pltpu.VMEM), out_shape
        ),
        scratch_shapes=list(scratch),
        compiler_params=pltpu.CompilerParams(vmem_limit_bytes=limit),
        cost_estimate=pl.CostEstimate(flops=flops, bytes_accessed=size, transcendentals=0),
    )(*args)


def shape(s, d=F32):
    return jax.ShapeDtypeStruct(s, d)


def expm1(x):
    series = x * (1 + x * (1 / 2) * (1 + x * (1 / 3) * (1 + x * (1 / 4) * (1 + x * (1 / 5) * (1 + x * (1 / 6) * (1 + x * (1 / 7)))))))
    return jnp.where(x > -0.35, series, jnp.exp(x) - 1.0)


def send_hot(send):
    return lanes([one_hot(lanes([send[4 * i + j : 4 * i + j + 1, :] for j in range(4)]), 256) for i in range(8)])


def k_send(features_hbm, send_hbm, hub_hbm, out, features, send, hub, sems):
    pairs = ((features_hbm, features), (send_hbm, send), (hub_hbm, hub))
    copies = [pltpu.make_async_copy(src, dst, sems.at[n]) for n, (src, dst) in enumerate(pairs)]
    for copy in copies:
        copy.start()
    for copy in copies:
        copy.wait()
    x = halves(features[...])
    out[:, 0:32, :] = joined(dot(send_hot(send), x, TN)).reshape(32, 32, 128)
    hub_rows = joined(dot(one_hot(hub[...], 256), x, TN))
    for p in range(32):
        out[p, 32:40, :] = hub_rows


def k_lists(pos, coord, edge, hub_to, hub_from, own_to, *outs):
    me = pos[0]
    for b in range(8):
        for t in range(6):
            own_to[b * 6 + t : b * 6 + t + 1, :] = edge[b, t, 0:1, :] + coord[b, 0, t] * 128
    for d in range(2):
        for k in range(4):
            b = jnp.bitwise_xor(me // 4, d) * 4 + (me % 4 + k) % 4
            at = d * 16
            for t in range(6):
                outs[k][at + t : at + t + 1, :] = edge[b, t, 0:1, :] + coord[b, 0, t] * 128
                outs[k][at + 6 + t : at + 7 + t, :] = edge[b, t, 1:2, :] + coord[b, 1, t] * 128
            outs[k][at + 12 : at + 14, :] = hub_to[...]
            outs[k][at + 14 : at + 16, :] = hub_from[...]


def hots(pos, block):
    me = pos[0]
    to = lanes([one_hot(block[i : i + 1, :], 256) for i in range(6)])
    frm = lanes([one_hot(block[i : i + 1, :], 256) for i in range(6, 12)])
    h_to = lanes([one_hot(block[i : i + 1, :], 256) for i in range(12, 14)])
    codes = [block[i : i + 1, :] for i in range(14, 16)]
    rows = [jnp.where((c >> 3) % 8 == me, (c >> 6) * 8 + c % 8, -1) for c in codes]
    return to, frm, h_to, lanes([one_hot(c, 256) for c in rows])


def blocks_of(lists):
    own, l1, l2, l3, far = lists
    return [ref[0:16, :] for ref in (own, l1, l2, l3)] + [far[16 * k : 16 * k + 16, :] for k in range(4)]


def halo_hots(halo_to, halo_from):
    to = lanes([one_hot(halo_to[i : i + 1, :], 256) for i in range(8)])
    return to, lanes([one_hot(halo_from[i : i + 1, :], 1024) for i in range(8)])


def rest(count):
    return (count - count.astype(BF16).astype(F32)).astype(BF16)


def forward_count(to, frm, h_to, h_frm):
    return jnp.concatenate([dot(to, frm, NT), dot(h_to, h_frm, NT)], axis=1)


def backward_count(to, frm, h_to, h_frm):
    return jnp.concatenate([dot(frm, to, NT), dot(h_frm, h_to, NT)], axis=0)


def k_fwd(pos, l0, l1, l2, l3, far, fwd, flag):
    top = jnp.float32(0.0)
    for r, block in enumerate(blocks_of((l0, l1, l2, l3, far))):
        count = forward_count(*hots(pos, block))
        top = jnp.maximum(top, jnp.max(count))
        fwd[r] = count.astype(BF16)
    flag[0] = (top > 256.0).astype(I32)


def k_bwd(pos, l0, l1, l2, l3, far, bwd):
    for r, block in enumerate(blocks_of((l0, l1, l2, l3, far))):
        bwd[r] = backward_count(*hots(pos, block)).astype(BF16)


def k_boundary(own_to, halo_to, halo_from, hub_to, h_fwd, h_bwd, inv, flag):
    to, frm = halo_hots(halo_to, halo_from)
    count = dot(to, frm, NT)
    h_fwd[...] = count.astype(BF16)
    h_bwd[...] = dot(frm, to, NT).astype(BF16)
    flag[0] = (jnp.max(count) > 256.0).astype(I32)
    row = lax.broadcasted_iota(I32, (256, 128), 0)
    degree = jnp.zeros((256, 128), F32)
    for ref, n in ((own_to, 48), (halo_to, 8), (hub_to, 2)):
        for i in range(n):
            degree = degree + jnp.where(row == ref[i : i + 1, :], 1.0, 0.0)
    degree = jnp.sum(degree, axis=1, keepdims=True)
    inv[...] = jnp.broadcast_to(1.0 / (degree + 1.0), (256, 128))


def k_partial(flag, pos, l0, l1, l2, l3, far, features, incoming, fwd, *outs):
    hubs = incoming[:, 32:40, :].reshape(256, 128)
    x = jnp.concatenate([halves(features[...]), halves(hubs)], axis=0)
    for r in range(8):
        outs[r][...] = joined(dot(fwd[r], x))

    @pl.when(flag[0] != 0)
    def _():
        for r, block in enumerate(blocks_of((l0, l1, l2, l3, far))):
            outs[r][...] += joined(dot(rest(forward_count(*hots(pos, block))), x))


def k_halo(flag, halo_to, halo_from, incoming, h_fwd, own, out):
    x = halves(incoming[:, 0:32, :].reshape(1024, 128))
    out[...] = own[...] + joined(dot(h_fwd[...], x))

    @pl.when(flag[0] != 0)
    def _():
        to, frm = halo_hots(halo_to, halo_from)
        out[...] += joined(dot(rest(dot(to, frm, NT)), x))


def k_layer(a0, a1, a2, a3, a4, inv, features, w_neigh, w_root, bias, grad_out,
            output, grad_pre, grad_sum, mean):
    scale = inv[...]
    m = (a0[...] + a1[...] + a2[...] + a3[...] + a4[...]) * scale
    mean[...] = m
    pre = dot(m, w_neigh[...], NN, HIGH) + dot(features[...], w_root[...], NN, HIGH) + bias[...]
    negative = jnp.minimum(pre, 0.0)
    output[...] = jnp.where(pre > 0, pre, expm1(negative))
    g = grad_out[...] * jnp.where(pre > 0, 1.0, jnp.exp(negative))
    grad_pre[...] = g
    grad_sum[...] = dot(g, w_neigh[...], NT, HIGH) * scale


def spot(n):
    return pl.ds(pl.multiple_of(n * 8, 8), 8)


def k_weights(here, grad_pre, mean, features, own, other, held):
    c = here[0] % 2
    g = grad_pre[...]
    held[0:128, :] = dot(mean[...], g, TN, HIGH)
    held[128:256, :] = dot(features[...], g, TN, HIGH)
    fill = jnp.broadcast_to(jnp.sum(g, axis=0, keepdims=True), (8, 128))
    for d, out in enumerate((own, other)):
        for n in range(16):
            out[n * 8 : n * 8 + 8, :] = held[spot(n * 2 + jnp.bitwise_xor(c, d)), :]
        out[128:136, :] = fill


def k_over_core(here, a, b, o0, o1, o2, o3, held):
    x = here[0] // 2 % 4
    held[...] = a[...] + b[...]
    for k, out in enumerate((o0, o1, o2, o3)):
        for n in range(4):
            out[n * 8 : n * 8 + 8, :] = held[spot(n * 4 + (x + k) % 4), :]
        out[32:40, :] = held[128:136, :]


def k_over_x(here, a, b, c, d, o0, o1, o2, o3, held):
    held[...] = a[...] + b[...] + c[...] + d[...]
    for m, out in enumerate((o0, o1, o2, o3)):
        out[0:8, :] = held[spot(jnp.bitwise_xor(here[0] // 8, m)), :]
        out[8:16, :] = held[32:40, :]


def k_sum(a, b, c, d, out):
    out[...] = a[...] + b[...] + c[...] + d[...]


def k_slots(flag, halo_to, halo_from, grad_sum, h_bwd, out):
    x = halves(grad_sum[...])
    out[...] = joined(dot(h_bwd[...], x))

    @pl.when(flag[0] != 0)
    def _():
        to, frm = halo_hots(halo_to, halo_from)
        out[...] += joined(dot(rest(dot(frm, to, NT)), x))


def k_back(flag, pos, l0, l1, l2, l3, far, g0, g1, g2, g3, g4, g5, g6, g7, bwd, local, hubs, total):
    xs = [halves(g[0:256, :]) for g in (g0, g1, g2, g3, g4, g5, g6, g7)]
    acc = dot(bwd[0], xs[0])
    for r in range(1, 8):
        acc = acc + dot(bwd[r], xs[r])
    total[...] = joined(acc)

    @pl.when(flag[0] != 0)
    def _():
        for r, block in enumerate(blocks_of((l0, l1, l2, l3, far))):
            total[...] += joined(dot(rest(backward_count(*hots(pos, block))), xs[r]))

    hubs[...] = total[256:512, :].reshape(32, 8, 128)
    local[...] = total[0:256, :]


def k_pack(factor, hubs, near, far, out, bias):
    w = (near[...] + far[...]) * factor
    out[:, 0:8, :] = hubs[...]
    for p in range(32):
        out[p, 8:16, :] = w[0:8]
    bias[...] = w[8:9]


def k_scatter(returned, send, local, grad_pre, w_root, out):
    root = dot(grad_pre[...], w_root[...], NT, HIGH)
    out[...] = local[...] + root + joined(dot(send_hot(send), halves(returned[...].reshape(1024, 128))))


def k_final(last, hub, local, out, w_neigh, w_root):
    rows = jnp.sum(last[:, 0:8, :], axis=0)
    out[...] = local[...]
    for j in range(8):
        out[pl.ds(hub[j], 1), :] += rows[j : j + 1, :]
    w_neigh[...] = last[0:16, 8:16, :].reshape(128, 128)
    w_root[...] = last[16:32, 8:16, :].reshape(128, 128)


def per_device(features, w_neigh, w_root, bias, grad_out, tile_coord, tile_edge,
               send_idx, halo_dst, halo_src, hub_idx, hub_dst, hub_src):
    send = send_idx.reshape(32, 32)
    hub = hub_idx.reshape(8)
    hub_to = hub_dst.reshape(2, 128)
    hub_from = hub_src.reshape(2, 128)
    halo_to = halo_dst.reshape(8, 128)
    halo_from = halo_src.reshape(8, 128)
    pos = lax.axis_index("blk").astype(I32).reshape(1)
    block = shape((256, 128))

    def swap(v):
        return lax.ppermute(v, "blk", [(i, i ^ 4) for i in range(8)])

    def turn(v, k):
        return lax.ppermute(v, "blk", [(i, i // 4 * 4 + (i % 4 + k) % 4) for i in range(8)])

    def exchange(v, axis):
        return lax.all_to_all(v, axis, split_axis=0, concat_axis=0, tiled=True)

    vm, sm, hb = (pl.BlockSpec(memory_space=s) for s in (pltpu.VMEM, pltpu.SMEM, pltpu.HBM))

    outgoing = call(
        k_send, shape((32, 40, 128)), (features, send, hub_idx.reshape(1, 8)), [hb] * 3,
        [pltpu.VMEM((256, 128), F32), pltpu.VMEM((32, 32), I32), pltpu.VMEM((1, 8), I32), pltpu.SemaphoreType.DMA((3,))],
        limit=60 << 20,
    )
    outgoing, coord = lax.optimization_barrier((outgoing, tile_coord.reshape(8, 2, 6)))
    incoming = exchange(outgoing, "grp")
    own_to, m0, m1, m2, m3 = call(
        k_lists, [shape((48, 128), I32)] + [shape((32, 128), I32)] * 4,
        (pos, coord, tile_edge.reshape(8, 6, 2, 128), hub_to, hub_from), [sm, sm, vm, vm, vm],
    )
    l3, l2, l1 = turn(m1, 1), turn(m2, 2), turn(m3, 3)
    far = swap(jnp.concatenate([m0[16:], l1[16:], l2[16:], l3[16:]], axis=0))
    lists = (pos, m0, l1, l2, l3, far)
    lm = [sm] + [vm] * 5
    h_fwd, h_bwd, inv, h_flag = call(
        k_boundary, (shape((256, 1024), BF16), shape((1024, 256), BF16), block, shape((1,), I32)),
        (own_to, halo_to, halo_from, hub_to), flops=1 << 31,
    )
    fwd, flag = call(k_fwd, (shape((8, 256, 512), BF16), shape((1,), I32)), lists, lm, flops=1 << 31)
    bwd = call(k_bwd, shape((8, 512, 256), BF16), lists, lm, flops=1 << 31)
    part = call(k_partial, [block] * 8, (flag, *lists, features, incoming, fwd), [sm, *lm, vm, vm, vm])
    other = part[4] + turn(part[5], 1) + turn(part[7], 3) + turn(part[6], 2)
    other, p1, p2, p3 = lax.optimization_barrier((other, part[1], part[2], part[3]))
    other = swap(other)
    near = [turn(p1, 1), turn(p3, 3), turn(p2, 2)]
    own = call(k_halo, block, (h_flag, halo_to, halo_from, incoming, h_fwd, part[0]), [sm] + [vm] * 5)
    inv, bwd = lax.optimization_barrier((inv, bwd))
    output, grad_pre, grad_sum, mean = call(
        k_layer, [block] * 4, (own, other, *near, inv, features, w_neigh, w_root, bias.reshape(1, 128), grad_out),
    )
    g4 = swap(grad_sum)
    g1, g3, g2 = turn(grad_sum, 3), turn(grad_sum, 1), turn(grad_sum, 2)
    slots = call(k_slots, shape((1024, 128)), (h_flag, halo_to, halo_from, grad_sum, h_bwd), [sm] + [vm] * 4)
    returned = exchange(slots.reshape(32, 32, 128), "grp")
    here = lax.axis_index("grp").astype(I32).reshape(1)

    def move(v, to):
        return lax.ppermute(v, "grp", [(i, to(i)) for i in range(32)])

    mine, others = call(
        k_weights, [shape((136, 128))] * 2, (here, grad_pre, mean, features), [sm, vm, vm, vm], [pltpu.VMEM((256, 128), F32)]
    )
    cut = call(
        k_over_core, [shape((40, 128))] * 4, (here, mine, move(others, lambda i: i ^ 1)), [sm, vm, vm],
        [pltpu.VMEM((136, 128), F32)],
    )
    spun = [move(cut[k], lambda i: i // 8 * 8 + (i % 8 + 2 * k) % 8) for k in (1, 2, 3)]
    cut = call(
        k_over_x, [shape((16, 128))] * 4, (here, cut[0], *spun), [sm] + [vm] * 4, [pltpu.VMEM((40, 128), F32)]
    )
    w = call(k_sum, shape((16, 128)), (cut[0], *[move(cut[m], lambda i: i ^ (8 * m)) for m in (1, 2, 3)]))
    w = call(k_sum, shape((16, 128)), (w, turn(w, 1), turn(w, 2), turn(w, 3)))
    w_far = swap(w)
    g5, g7, g6 = turn(g4, 3), turn(g4, 1), turn(g4, 2)
    local, hubs = call(
        k_back, [block, shape((32, 8, 128))],
        (flag, *lists, grad_sum, g1, g2, g3, g4, g5, g6, g7, bwd), [sm, *lm] + [vm] * 9,
        [pltpu.VMEM((512, 128), F32)],
    )
    factor = (256 * lax.axis_size("grp") * lax.axis_size("blk")) ** (-0.5)
    last, grad_bias = call(
        functools.partial(k_pack, factor), [shape((32, 16, 128)), shape((1, 128))], (hubs, w, w_far)
    )
    last = exchange(last, "grp")
    local = call(k_scatter, block, (returned, send, local, grad_pre, w_root))
    grad_features, grad_wn, grad_wr = call(
        k_final, [block, shape((128, 128)), shape((128, 128))], (last, hub, local), [vm, sm, vm]
    )
    return output, grad_features, grad_wn, grad_wr, grad_bias.reshape(128)


def solution(mesh):
    rows = P(("grp", "blk"), None)
    in_specs = (
        rows, P(), P(), P(), rows,
        P("grp", "blk", None, None, None),
        P("grp", "blk", None, None, None, None),
        P("grp", "blk", None, None),
        P("grp", "blk", None), P("grp", "blk", None), P("grp", "blk", None), P("grp", "blk", None), P("grp", "blk", None),
    )
    return jax.shard_map(
        per_device, mesh=mesh, in_specs=in_specs, out_specs=(rows, rows, P(), P(), P()), check_vma=False
    )
```

```python
import functools

import jax
import jax.numpy as jnp
from jax import lax
from jax.experimental import pallas as pl
from jax.experimental.pallas import tpu as pltpu
from jax.sharding import PartitionSpec as P

HIGH = lax.Precision.HIGHEST
F32, BF16, I32 = jnp.float32, jnp.bfloat16, jnp.int32
NT = (((1,), (1,)), ((), ()))
NN = (((1,), (0,)), ((), ()))
TN = (((0,), (0,)), ((), ()))


def dot(a, b, dims=NN, precision=None):
    return lax.dot_general(a, b, dims, precision=precision, preferred_element_type=F32)


def halves(x):
    high = x.astype(BF16)
    low = (x - high.astype(F32)).astype(BF16)
    return jnp.concatenate([high, low], axis=1)


def joined(y):
    n = y.shape[1] // 2
    return y[:, :n] + y[:, n:]


def one_hot(idx, rows):
    n = idx.shape[1]
    row = lax.broadcasted_iota(I32, (rows, n), 0)
    return jnp.where(row == idx, 1.0, 0.0).astype(BF16)


def lanes(ref_rows):
    return jnp.concatenate(ref_rows, axis=1)


def call(kernel, out_shape, args, specs=None, scratch=(), flops=1 << 28, limit=16 << 20):
    whole = pl.BlockSpec(memory_space=pltpu.VMEM)
    size = sum(int(a.size) * a.dtype.itemsize for a in args)
    return pl.pallas_call(
        kernel,
        out_shape=out_shape,
        in_specs=[whole] * len(args) if specs is None else specs,
        out_specs=jax.tree.map(
            lambda s: pl.BlockSpec(memory_space=pltpu.SMEM if s.shape == (1,) else pltpu.VMEM), out_shape
        ),
        scratch_shapes=list(scratch),
        compiler_params=pltpu.CompilerParams(vmem_limit_bytes=limit),
        cost_estimate=pl.CostEstimate(flops=flops, bytes_accessed=size, transcendentals=0),
    )(*args)


def shape(s, d=F32):
    return jax.ShapeDtypeStruct(s, d)


def expm1(x):
    series = x * (1 + x * (1 / 2) * (1 + x * (1 / 3) * (1 + x * (1 / 4) * (1 + x * (1 / 5) * (1 + x * (1 / 6) * (1 + x * (1 / 7)))))))
    return jnp.where(x > -0.35, series, jnp.exp(x) - 1.0)


def send_hot(send):
    return lanes([one_hot(lanes([send[4 * i + j : 4 * i + j + 1, :] for j in range(4)]), 256) for i in range(8)])


def k_send(features_hbm, send_hbm, hub_hbm, out, features, send, hub, sems):
    pairs = ((features_hbm, features), (send_hbm, send), (hub_hbm, hub))
    copies = [pltpu.make_async_copy(src, dst, sems.at[n]) for n, (src, dst) in enumerate(pairs)]
    for copy in copies:
        copy.start()
    for copy in copies:
        copy.wait()
    x = halves(features[...])
    out[:, 0:32, :] = joined(dot(send_hot(send), x, TN)).reshape(32, 32, 128)
    hub_rows = joined(dot(one_hot(hub[...], 256), x, TN))
    for p in range(32):
        out[p, 32:40, :] = hub_rows


def k_lists(pos, coord, edge, hub_to, hub_from, own_to, *outs):
    me = pos[0]
    for b in range(8):
        for t in range(6):
            own_to[b * 6 + t : b * 6 + t + 1, :] = edge[b, t, 0:1, :] + coord[b, 0, t] * 128
    for d in range(2):
        for k in range(4):
            b = jnp.bitwise_xor(me // 4, d) * 4 + (me % 4 + k) % 4
            at = d * 16
            for t in range(6):
                outs[k][at + t : at + t + 1, :] = edge[b, t, 0:1, :] + coord[b, 0, t] * 128
                outs[k][at + 6 + t : at + 7 + t, :] = edge[b, t, 1:2, :] + coord[b, 1, t] * 128
            outs[k][at + 12 : at + 14, :] = hub_to[...]
            outs[k][at + 14 : at + 16, :] = hub_from[...]


def hots(pos, block):
    me = pos[0]
    to = lanes([one_hot(block[i : i + 1, :], 256) for i in range(6)])
    frm = lanes([one_hot(block[i : i + 1, :], 256) for i in range(6, 12)])
    h_to = lanes([one_hot(block[i : i + 1, :], 256) for i in range(12, 14)])
    codes = [block[i : i + 1, :] for i in range(14, 16)]
    rows = [jnp.where((c >> 3) % 8 == me, (c >> 6) * 8 + c % 8, -1) for c in codes]
    return to, frm, h_to, lanes([one_hot(c, 256) for c in rows])


def blocks_of(lists):
    own, l1, l2, l3, far = lists
    return [ref[0:16, :] for ref in (own, l1, l2, l3)] + [far[16 * k : 16 * k + 16, :] for k in range(4)]


def halo_hots(halo_to, halo_from):
    to = lanes([one_hot(halo_to[i : i + 1, :], 256) for i in range(8)])
    return to, lanes([one_hot(halo_from[i : i + 1, :], 1024) for i in range(8)])


def rest(count):
    return (count - count.astype(BF16).astype(F32)).astype(BF16)


def forward_count(to, frm, h_to, h_frm):
    return jnp.concatenate([dot(to, frm, NT), dot(h_to, h_frm, NT)], axis=1)


def backward_count(to, frm, h_to, h_frm):
    return jnp.concatenate([dot(frm, to, NT), dot(h_frm, h_to, NT)], axis=0)


def k_fwd(pos, l0, l1, l2, l3, far, fwd, flag):
    top = jnp.float32(0.0)
    for r, block in enumerate(blocks_of((l0, l1, l2, l3, far))):
        count = forward_count(*hots(pos, block))
        top = jnp.maximum(top, jnp.max(count))
        fwd[r] = count.astype(BF16)
    flag[0] = (top > 256.0).astype(I32)


def k_bwd(pos, l0, l1, l2, l3, far, bwd):
    for r, block in enumerate(blocks_of((l0, l1, l2, l3, far))):
        bwd[r] = backward_count(*hots(pos, block)).astype(BF16)


def k_boundary(own_to, halo_to, halo_from, hub_to, h_fwd, h_bwd, inv, flag):
    to, frm = halo_hots(halo_to, halo_from)
    count = dot(to, frm, NT)
    h_fwd[...] = count.astype(BF16)
    h_bwd[...] = dot(frm, to, NT).astype(BF16)
    flag[0] = (jnp.max(count) > 256.0).astype(I32)
    row = lax.broadcasted_iota(I32, (256, 128), 0)
    degree = jnp.zeros((256, 128), F32)
    for ref, n in ((own_to, 48), (halo_to, 8), (hub_to, 2)):
        for i in range(n):
            degree = degree + jnp.where(row == ref[i : i + 1, :], 1.0, 0.0)
    degree = jnp.sum(degree, axis=1, keepdims=True)
    inv[...] = jnp.broadcast_to(1.0 / (degree + 1.0), (256, 128))


def k_partial(flag, pos, l0, l1, l2, l3, far, features, incoming, fwd, *outs):
    hubs = incoming[:, 32:40, :].reshape(256, 128)
    x = jnp.concatenate([halves(features[...]), halves(hubs)], axis=0)
    for r in range(8):
        outs[r][...] = joined(dot(fwd[r], x))

    @pl.when(flag[0] != 0)
    def _():
        for r, block in enumerate(blocks_of((l0, l1, l2, l3, far))):
            outs[r][...] += joined(dot(rest(forward_count(*hots(pos, block))), x))


def k_halo(flag, halo_to, halo_from, incoming, h_fwd, own, out):
    x = halves(incoming[:, 0:32, :].reshape(1024, 128))
    out[...] = own[...] + joined(dot(h_fwd[...], x))

    @pl.when(flag[0] != 0)
    def _():
        to, frm = halo_hots(halo_to, halo_from)
        out[...] += joined(dot(rest(dot(to, frm, NT)), x))


def k_layer(a0, a1, a2, a3, a4, inv, features, w_neigh, w_root, bias, grad_out,
            output, grad_pre, grad_sum, mean):
    scale = inv[...]
    m = (a0[...] + a1[...] + a2[...] + a3[...] + a4[...]) * scale
    mean[...] = m
    pre = dot(m, w_neigh[...], NN, HIGH) + dot(features[...], w_root[...], NN, HIGH) + bias[...]
    negative = jnp.minimum(pre, 0.0)
    output[...] = jnp.where(pre > 0, pre, expm1(negative))
    g = grad_out[...] * jnp.where(pre > 0, 1.0, jnp.exp(negative))
    grad_pre[...] = g
    grad_sum[...] = dot(g, w_neigh[...], NT, HIGH) * scale


def spot(n):
    return pl.ds(pl.multiple_of(n * 8, 8), 8)


def k_weights(here, grad_pre, mean, features, own, other, held):
    c = here[0] % 2
    g = grad_pre[...]
    held[0:128, :] = dot(mean[...], g, TN, HIGH)
    held[128:256, :] = dot(features[...], g, TN, HIGH)
    fill = jnp.broadcast_to(jnp.sum(g, axis=0, keepdims=True), (8, 128))
    for d, out in enumerate((own, other)):
        for n in range(16):
            out[n * 8 : n * 8 + 8, :] = held[spot(n * 2 + jnp.bitwise_xor(c, d)), :]
        out[128:136, :] = fill


def k_over_core(here, a, b, o0, o1, o2, o3, held):
    x = here[0] // 2 % 4
    held[...] = a[...] + b[...]
    for k, out in enumerate((o0, o1, o2, o3)):
        for n in range(4):
            out[n * 8 : n * 8 + 8, :] = held[spot(n * 4 + (x + k) % 4), :]
        out[32:40, :] = held[128:136, :]


def k_over_x(here, a, b, c, d, o0, o1, o2, o3, held):
    held[...] = a[...] + b[...] + c[...] + d[...]
    for m, out in enumerate((o0, o1, o2, o3)):
        out[0:8, :] = held[spot(jnp.bitwise_xor(here[0] // 8, m)), :]
        out[8:16, :] = held[32:40, :]


def k_sum(a, b, c, d, out):
    out[...] = a[...] + b[...] + c[...] + d[...]


def k_slots(flag, halo_to, halo_from, grad_sum, h_bwd, out):
    x = halves(grad_sum[...])
    out[...] = joined(dot(h_bwd[...], x))

    @pl.when(flag[0] != 0)
    def _():
        to, frm = halo_hots(halo_to, halo_from)
        out[...] += joined(dot(rest(dot(frm, to, NT)), x))


def k_back(flag, pos, l0, l1, l2, l3, far, g0, g1, g2, g3, g4, g5, g6, g7, bwd, local, hubs, total):
    xs = [halves(g[0:256, :]) for g in (g0, g1, g2, g3, g4, g5, g6, g7)]
    acc = dot(bwd[0], xs[0])
    for r in range(1, 8):
        acc = acc + dot(bwd[r], xs[r])
    total[...] = joined(acc)

    @pl.when(flag[0] != 0)
    def _():
        for r, block in enumerate(blocks_of((l0, l1, l2, l3, far))):
            total[...] += joined(dot(rest(backward_count(*hots(pos, block))), xs[r]))

    hubs[...] = total[256:512, :].reshape(32, 8, 128)
    local[...] = total[0:256, :]


def k_pack(factor, hubs, near, far, out, bias):
    w = (near[...] + far[...]) * factor
    out[:, 0:8, :] = hubs[...]
    for p in range(32):
        out[p, 8:16, :] = w[0:8]
    bias[...] = w[8:9]


def k_scatter(returned, send, local, grad_pre, w_root, out):
    root = dot(grad_pre[...], w_root[...], NT, HIGH)
    out[...] = local[...] + root + joined(dot(send_hot(send), halves(returned[...].reshape(1024, 128))))


def k_final(last, hub, local, out, w_neigh, w_root):
    rows = jnp.sum(last[:, 0:8, :], axis=0)
    out[...] = local[...]
    for j in range(8):
        out[pl.ds(hub[j], 1), :] += rows[j : j + 1, :]
    w_neigh[...] = last[0:16, 8:16, :].reshape(128, 128)
    w_root[...] = last[16:32, 8:16, :].reshape(128, 128)


def per_device(features, w_neigh, w_root, bias, grad_out, tile_coord, tile_edge,
               send_idx, halo_dst, halo_src, hub_idx, hub_dst, hub_src):
    send = send_idx.reshape(32, 32)
    hub = hub_idx.reshape(8)
    hub_to = hub_dst.reshape(2, 128)
    hub_from = hub_src.reshape(2, 128)
    halo_to = halo_dst.reshape(8, 128)
    halo_from = halo_src.reshape(8, 128)
    pos = lax.axis_index("blk").astype(I32).reshape(1)
    block = shape((256, 128))

    def swap(v):
        return lax.ppermute(v, "blk", [(i, i ^ 4) for i in range(8)])

    def turn(v, k):
        return lax.ppermute(v, "blk", [(i, i // 4 * 4 + (i % 4 + k) % 4) for i in range(8)])

    def exchange(v, axis):
        return lax.all_to_all(v, axis, split_axis=0, concat_axis=0, tiled=True)

    vm, sm, hb = (pl.BlockSpec(memory_space=s) for s in (pltpu.VMEM, pltpu.SMEM, pltpu.HBM))

    outgoing = call(
        k_send, shape((32, 40, 128)), (features, send, hub_idx.reshape(1, 8)), [hb] * 3,
        [pltpu.VMEM((256, 128), F32), pltpu.VMEM((32, 32), I32), pltpu.VMEM((1, 8), I32), pltpu.SemaphoreType.DMA((3,))],
        limit=60 << 20,
    )
    outgoing, coord = lax.optimization_barrier((outgoing, tile_coord.reshape(8, 2, 6)))
    incoming = exchange(outgoing, "grp")
    own_to, m0, m1, m2, m3 = call(
        k_lists, [shape((48, 128), I32)] + [shape((32, 128), I32)] * 4,
        (pos, coord, tile_edge.reshape(8, 6, 2, 128), hub_to, hub_from), [sm, sm, vm, vm, vm],
    )
    l3, l2, l1 = turn(m1, 1), turn(m2, 2), turn(m3, 3)
    far = swap(jnp.concatenate([m0[16:], l1[16:], l2[16:], l3[16:]], axis=0))
    lists = (pos, m0, l1, l2, l3, far)
    lm = [sm] + [vm] * 5
    h_fwd, h_bwd, inv, h_flag = call(
        k_boundary, (shape((256, 1024), BF16), shape((1024, 256), BF16), block, shape((1,), I32)),
        (own_to, halo_to, halo_from, hub_to), flops=1 << 31,
    )
    fwd, flag = call(k_fwd, (shape((8, 256, 512), BF16), shape((1,), I32)), lists, lm, flops=1 << 31)
    bwd = call(k_bwd, shape((8, 512, 256), BF16), lists, lm, flops=1 << 31)
    part = call(k_partial, [block] * 8, (flag, *lists, features, incoming, fwd), [sm, *lm, vm, vm, vm])
    other = part[4] + turn(part[5], 1) + turn(part[7], 3) + turn(part[6], 2)
    other, p1, p2, p3 = lax.optimization_barrier((other, part[1], part[2], part[3]))
    other = swap(other)
    near = [turn(p1, 1), turn(p3, 3), turn(p2, 2)]
    own = call(k_halo, block, (h_flag, halo_to, halo_from, incoming, h_fwd, part[0]), [sm] + [vm] * 5)
    inv, bwd = lax.optimization_barrier((inv, bwd))
    output, grad_pre, grad_sum, mean = call(
        k_layer, [block] * 4, (own, other, *near, inv, features, w_neigh, w_root, bias.reshape(1, 128), grad_out),
    )
    g4 = swap(grad_sum)
    g1, g3, g2 = turn(grad_sum, 3), turn(grad_sum, 1), turn(grad_sum, 2)
    slots = call(k_slots, shape((1024, 128)), (h_flag, halo_to, halo_from, grad_sum, h_bwd), [sm] + [vm] * 4)
    returned = exchange(slots.reshape(32, 32, 128), "grp")
    here = lax.axis_index("grp").astype(I32).reshape(1)

    def move(v, to):
        return lax.ppermute(v, "grp", [(i, to(i)) for i in range(32)])

    mine, others = call(
        k_weights, [shape((136, 128))] * 2, (here, grad_pre, mean, features), [sm, vm, vm, vm], [pltpu.VMEM((256, 128), F32)]
    )
    cut = call(
        k_over_core, [shape((40, 128))] * 4, (here, mine, move(others, lambda i: i ^ 1)), [sm, vm, vm],
        [pltpu.VMEM((136, 128), F32)],
    )
    spun = [move(cut[k], lambda i: i // 8 * 8 + (i % 8 + 2 * k) % 8) for k in (1, 2, 3)]
    cut = call(
        k_over_x, [shape((16, 128))] * 4, (here, cut[0], *spun), [sm] + [vm] * 4, [pltpu.VMEM((40, 128), F32)]
    )
    cut, g1, g2, g3 = lax.optimization_barrier((cut, g1, g2, g3))
    w = call(k_sum, shape((16, 128)), (cut[0], *[move(cut[m], lambda i: i ^ (8 * m)) for m in (1, 2, 3)]))
    w = call(k_sum, shape((16, 128)), (w, turn(w, 1), turn(w, 2), turn(w, 3)))
    w_far = swap(w)
    g5, g7, g6 = turn(g4, 3), turn(g4, 1), turn(g4, 2)
    local, hubs = call(
        k_back, [block, shape((32, 8, 128))],
        (flag, *lists, grad_sum, g1, g2, g3, g4, g5, g6, g7, bwd), [sm, *lm] + [vm] * 9,
        [pltpu.VMEM((512, 128), F32)],
    )
    factor = (256 * lax.axis_size("grp") * lax.axis_size("blk")) ** (-0.5)
    last, grad_bias = call(
        functools.partial(k_pack, factor), [shape((32, 16, 128)), shape((1, 128))], (hubs, w, w_far)
    )
    last = exchange(last, "grp")
    local = call(k_scatter, block, (returned, send, local, grad_pre, w_root))
    grad_features, grad_wn, grad_wr = call(
        k_final, [block, shape((128, 128)), shape((128, 128))], (last, hub, local), [vm, sm, vm]
    )
    return output, grad_features, grad_wn, grad_wr, grad_bias.reshape(128)


def solution(mesh):
    rows = P(("grp", "blk"), None)
    in_specs = (
        rows, P(), P(), P(), rows,
        P("grp", "blk", None, None, None),
        P("grp", "blk", None, None, None, None),
        P("grp", "blk", None, None),
        P("grp", "blk", None), P("grp", "blk", None), P("grp", "blk", None), P("grp", "blk", None), P("grp", "blk", None),
    )
    return jax.shard_map(
        per_device, mesh=mesh, in_specs=in_specs, out_specs=(rows, rows, P(), P(), P()), check_vma=False
    )
```

```python
import functools

import jax
import jax.numpy as jnp
from jax import lax
from jax.experimental import pallas as pl
from jax.experimental.pallas import tpu as pltpu
from jax.sharding import PartitionSpec as P

HIGH = lax.Precision.HIGHEST
F32, BF16, I32 = jnp.float32, jnp.bfloat16, jnp.int32
NT = (((1,), (1,)), ((), ()))
NN = (((1,), (0,)), ((), ()))
TN = (((0,), (0,)), ((), ()))


def dot(a, b, dims=NN, precision=None):
    return lax.dot_general(a, b, dims, precision=precision, preferred_element_type=F32)


def halves(x):
    high = x.astype(BF16)
    low = (x - high.astype(F32)).astype(BF16)
    return jnp.concatenate([high, low], axis=1)


def joined(y):
    n = y.shape[1] // 2
    return y[:, :n] + y[:, n:]


def one_hot(idx, rows):
    n = idx.shape[1]
    row = lax.broadcasted_iota(I32, (rows, n), 0)
    return jnp.where(row == idx, 1.0, 0.0).astype(BF16)


def lanes(ref_rows):
    return jnp.concatenate(ref_rows, axis=1)


def call(kernel, out_shape, args, specs=None, scratch=(), flops=1 << 28, limit=16 << 20):
    whole = pl.BlockSpec(memory_space=pltpu.VMEM)
    size = sum(int(a.size) * a.dtype.itemsize for a in args)
    return pl.pallas_call(
        kernel,
        out_shape=out_shape,
        in_specs=[whole] * len(args) if specs is None else specs,
        out_specs=jax.tree.map(
            lambda s: pl.BlockSpec(memory_space=pltpu.SMEM if s.shape == (1,) else pltpu.VMEM), out_shape
        ),
        scratch_shapes=list(scratch),
        compiler_params=pltpu.CompilerParams(vmem_limit_bytes=limit),
        cost_estimate=pl.CostEstimate(flops=flops, bytes_accessed=size, transcendentals=0),
    )(*args)


def shape(s, d=F32):
    return jax.ShapeDtypeStruct(s, d)


def expm1(x):
    series = x * (1 + x * (1 / 2) * (1 + x * (1 / 3) * (1 + x * (1 / 4) * (1 + x * (1 / 5) * (1 + x * (1 / 6) * (1 + x * (1 / 7)))))))
    return jnp.where(x > -0.35, series, jnp.exp(x) - 1.0)


def send_hot(send):
    return lanes([one_hot(lanes([send[4 * i + j : 4 * i + j + 1, :] for j in range(4)]), 256) for i in range(8)])


def k_send(features_hbm, send_hbm, hub_hbm, out, features, send, hub, sems):
    pairs = ((features_hbm, features), (send_hbm, send), (hub_hbm, hub))
    copies = [pltpu.make_async_copy(src, dst, sems.at[n]) for n, (src, dst) in enumerate(pairs)]
    for copy in copies:
        copy.start()
    for copy in copies:
        copy.wait()
    x = halves(features[...])
    out[:, 0:32, :] = joined(dot(send_hot(send), x, TN)).reshape(32, 32, 128)
    hub_rows = joined(dot(one_hot(hub[...], 256), x, TN))
    for p in range(32):
        out[p, 32:40, :] = hub_rows


def k_lists(pos, coord, edge, hub_to, hub_from, own_to, *outs):
    me = pos[0]
    for b in range(8):
        for t in range(6):
            own_to[b * 6 + t : b * 6 + t + 1, :] = edge[b, t, 0:1, :] + coord[b, 0, t] * 128
    for d in range(2):
        for k in range(4):
            b = jnp.bitwise_xor(me // 4, d) * 4 + (me % 4 + k) % 4
            at = d * 16
            for t in range(6):
                outs[k][at + t : at + t + 1, :] = edge[b, t, 0:1, :] + coord[b, 0, t] * 128
                outs[k][at + 6 + t : at + 7 + t, :] = edge[b, t, 1:2, :] + coord[b, 1, t] * 128
            outs[k][at + 12 : at + 14, :] = hub_to[...]
            outs[k][at + 14 : at + 16, :] = hub_from[...]


def hots(pos, block):
    me = pos[0]
    to = lanes([one_hot(block[i : i + 1, :], 256) for i in range(6)])
    frm = lanes([one_hot(block[i : i + 1, :], 256) for i in range(6, 12)])
    h_to = lanes([one_hot(block[i : i + 1, :], 256) for i in range(12, 14)])
    codes = [block[i : i + 1, :] for i in range(14, 16)]
    rows = [jnp.where((c >> 3) % 8 == me, (c >> 6) * 8 + c % 8, -1) for c in codes]
    return to, frm, h_to, lanes([one_hot(c, 256) for c in rows])


def blocks_of(lists):
    own, l1, l2, l3, far = lists
    return [ref[0:16, :] for ref in (own, l1, l2, l3)] + [far[16 * k : 16 * k + 16, :] for k in range(4)]


def halo_hots(halo_to, halo_from):
    to = lanes([one_hot(halo_to[i : i + 1, :], 256) for i in range(8)])
    return to, lanes([one_hot(halo_from[i : i + 1, :], 1024) for i in range(8)])


def rest(count):
    return (count - count.astype(BF16).astype(F32)).astype(BF16)


def forward_count(to, frm, h_to, h_frm):
    return jnp.concatenate([dot(to, frm, NT), dot(h_to, h_frm, NT)], axis=1)


def backward_count(to, frm, h_to, h_frm):
    return jnp.concatenate([dot(frm, to, NT), dot(h_frm, h_to, NT)], axis=0)


def k_fwd(pos, l0, l1, l2, l3, far, fwd, flag):
    top = jnp.float32(0.0)
    for r, block in enumerate(blocks_of((l0, l1, l2, l3, far))):
        count = forward_count(*hots(pos, block))
        top = jnp.maximum(top, jnp.max(count))
        fwd[r] = count.astype(BF16)
    flag[0] = (top > 256.0).astype(I32)


def k_bwd(pos, l0, l1, l2, l3, far, bwd):
    for r, block in enumerate(blocks_of((l0, l1, l2, l3, far))):
        bwd[r] = backward_count(*hots(pos, block)).astype(BF16)


def k_boundary(own_to, halo_to, halo_from, hub_to, h_fwd, h_bwd, inv, flag):
    to, frm = halo_hots(halo_to, halo_from)
    count = dot(to, frm, NT)
    h_fwd[...] = count.astype(BF16)
    h_bwd[...] = dot(frm, to, NT).astype(BF16)
    flag[0] = (jnp.max(count) > 256.0).astype(I32)
    row = lax.broadcasted_iota(I32, (256, 128), 0)
    degree = jnp.zeros((256, 128), F32)
    for ref, n in ((own_to, 48), (halo_to, 8), (hub_to, 2)):
        for i in range(n):
            degree = degree + jnp.where(row == ref[i : i + 1, :], 1.0, 0.0)
    degree = jnp.sum(degree, axis=1, keepdims=True)
    inv[...] = jnp.broadcast_to(1.0 / (degree + 1.0), (256, 128))


def k_partial(flag, pos, l0, l1, l2, l3, far, features, incoming, fwd, *outs):
    hubs = incoming[:, 32:40, :].reshape(256, 128)
    x = jnp.concatenate([halves(features[...]), halves(hubs)], axis=0)
    for r in range(8):
        outs[r][...] = joined(dot(fwd[r], x))

    @pl.when(flag[0] != 0)
    def _():
        for r, block in enumerate(blocks_of((l0, l1, l2, l3, far))):
            outs[r][...] += joined(dot(rest(forward_count(*hots(pos, block))), x))


def k_halo(flag, halo_to, halo_from, incoming, h_fwd, own, out):
    x = halves(incoming[:, 0:32, :].reshape(1024, 128))
    out[...] = own[...] + joined(dot(h_fwd[...], x))

    @pl.when(flag[0] != 0)
    def _():
        to, frm = halo_hots(halo_to, halo_from)
        out[...] += joined(dot(rest(dot(to, frm, NT)), x))


def k_layer(a0, a1, a2, a3, a4, inv, features, w_neigh, w_root, bias, grad_out,
            output, grad_pre, grad_sum, mean):
    scale = inv[...]
    m = (a0[...] + a1[...] + a2[...] + a3[...] + a4[...]) * scale
    mean[...] = m
    pre = dot(m, w_neigh[...], NN, HIGH) + dot(features[...], w_root[...], NN, HIGH) + bias[...]
    negative = jnp.minimum(pre, 0.0)
    output[...] = jnp.where(pre > 0, pre, expm1(negative))
    g = grad_out[...] * jnp.where(pre > 0, 1.0, jnp.exp(negative))
    grad_pre[...] = g
    grad_sum[...] = dot(g, w_neigh[...], NT, HIGH) * scale


def k_weights(grad_pre, mean, features, out):
    g = grad_pre[...]
    out[0:16, 0:8, :] = dot(mean[...], g, TN, HIGH).reshape(16, 8, 128)
    out[16:32, 0:8, :] = dot(features[...], g, TN, HIGH).reshape(16, 8, 128)
    fill = jnp.broadcast_to(jnp.sum(g, axis=0, keepdims=True), (8, 128))
    for p in range(32):
        out[p, 8:16, :] = fill


def k_slots(flag, halo_to, halo_from, grad_sum, h_bwd, out):
    x = halves(grad_sum[...])
    out[...] = joined(dot(h_bwd[...], x))

    @pl.when(flag[0] != 0)
    def _():
        to, frm = halo_hots(halo_to, halo_from)
        out[...] += joined(dot(rest(dot(frm, to, NT)), x))


def k_back(flag, pos, l0, l1, l2, l3, far, g0, g1, g2, g3, g4, g5, g6, g7, bwd, local, hubs, total):
    xs = [halves(g[0:256, :]) for g in (g0, g1, g2, g3, g4, g5, g6, g7)]
    acc = dot(bwd[0], xs[0])
    for r in range(1, 8):
        acc = acc + dot(bwd[r], xs[r])
    total[...] = joined(acc)

    @pl.when(flag[0] != 0)
    def _():
        for r, block in enumerate(blocks_of((l0, l1, l2, l3, far))):
            total[...] += joined(dot(rest(backward_count(*hots(pos, block))), xs[r]))

    hubs[...] = total[256:512, :].reshape(32, 8, 128)
    local[...] = total[0:256, :]


def k_sum(weights, out):
    out[...] = jnp.sum(weights[...], axis=0)


def k_pack(factor, hubs, near, far, out, bias):
    w = (near[...] + far[...]) * factor
    out[:, 0:8, :] = hubs[...]
    for p in range(32):
        out[p, 8:16, :] = w[0:8]
    bias[...] = w[8:9]


def k_scatter(returned, send, local, grad_pre, w_root, out):
    root = dot(grad_pre[...], w_root[...], NT, HIGH)
    out[...] = local[...] + root + joined(dot(send_hot(send), halves(returned[...].reshape(1024, 128))))


def k_final(last, hub, local, out, w_neigh, w_root):
    rows = jnp.sum(last[:, 0:8, :], axis=0)
    out[...] = local[...]
    for j in range(8):
        out[pl.ds(hub[j], 1), :] += rows[j : j + 1, :]
    w_neigh[...] = last[0:16, 8:16, :].reshape(128, 128)
    w_root[...] = last[16:32, 8:16, :].reshape(128, 128)


def per_device(features, w_neigh, w_root, bias, grad_out, tile_coord, tile_edge,
               send_idx, halo_dst, halo_src, hub_idx, hub_dst, hub_src):
    send = send_idx.reshape(32, 32)
    hub = hub_idx.reshape(8)
    hub_to = hub_dst.reshape(2, 128)
    hub_from = hub_src.reshape(2, 128)
    halo_to = halo_dst.reshape(8, 128)
    halo_from = halo_src.reshape(8, 128)
    pos = lax.axis_index("blk").astype(I32).reshape(1)
    block = shape((256, 128))

    def swap(v):
        return lax.ppermute(v, "blk", [(i, i ^ 4) for i in range(8)])

    def turn(v, k):
        return lax.ppermute(v, "blk", [(i, i // 4 * 4 + (i % 4 + k) % 4) for i in range(8)])

    def exchange(v, axis):
        return lax.all_to_all(v, axis, split_axis=0, concat_axis=0, tiled=True)

    vm, sm, hb = (pl.BlockSpec(memory_space=s) for s in (pltpu.VMEM, pltpu.SMEM, pltpu.HBM))

    outgoing = call(
        k_send, shape((32, 40, 128)), (features, send, hub_idx.reshape(1, 8)), [hb] * 3,
        [pltpu.VMEM((256, 128), F32), pltpu.VMEM((32, 32), I32), pltpu.VMEM((1, 8), I32), pltpu.SemaphoreType.DMA((3,))],
        limit=60 << 20,
    )
    outgoing, coord = lax.optimization_barrier((outgoing, tile_coord.reshape(8, 2, 6)))
    incoming = exchange(outgoing, "grp")
    own_to, m0, m1, m2, m3 = call(
        k_lists, [shape((48, 128), I32)] + [shape((32, 128), I32)] * 4,
        (pos, coord, tile_edge.reshape(8, 6, 2, 128), hub_to, hub_from), [sm, sm, vm, vm, vm],
    )
    l3, l2, l1 = turn(m1, 1), turn(m2, 2), turn(m3, 3)
    far = swap(jnp.concatenate([m0[16:], l1[16:], l2[16:], l3[16:]], axis=0))
    lists = (pos, m0, l1, l2, l3, far)
    lm = [sm] + [vm] * 5
    h_fwd, h_bwd, inv, h_flag = call(
        k_boundary, (shape((256, 1024), BF16), shape((1024, 256), BF16), block, shape((1,), I32)),
        (own_to, halo_to, halo_from, hub_to), flops=1 << 31,
    )
    fwd, flag = call(k_fwd, (shape((8, 256, 512), BF16), shape((1,), I32)), lists, lm, flops=1 << 31)
    bwd = call(k_bwd, shape((8, 512, 256), BF16), lists, lm, flops=1 << 31)
    part = call(k_partial, [block] * 8, (flag, *lists, features, incoming, fwd), [sm, *lm, vm, vm, vm])
    other = part[4] + turn(part[5], 1) + turn(part[7], 3) + turn(part[6], 2)
    other, p1, p2, p3 = lax.optimization_barrier((other, part[1], part[2], part[3]))
    other = swap(other)
    near = [turn(p2, 2), turn(p1, 1), turn(p3, 3)]
    own = call(k_halo, block, (h_flag, halo_to, halo_from, incoming, h_fwd, part[0]), [sm] + [vm] * 5)
    inv, bwd = lax.optimization_barrier((inv, bwd))
    output, grad_pre, grad_sum, mean = call(
        k_layer, [block] * 4, (own, other, *near, inv, features, w_neigh, w_root, bias.reshape(1, 128), grad_out),
    )
    g4 = swap(grad_sum)
    g1, g3, g2 = turn(grad_sum, 3), turn(grad_sum, 1), turn(grad_sum, 2)
    weights = exchange(call(k_weights, shape((32, 16, 128)), (grad_pre, mean, features)), "grp")
    slots = call(k_slots, shape((1024, 128)), (h_flag, halo_to, halo_from, grad_sum, h_bwd), [sm] + [vm] * 4)
    g4, weights, g1, g2, g3, slots = lax.optimization_barrier((g4, weights, g1, g2, g3, slots))
    returned = exchange(slots.reshape(32, 32, 128), "grp")
    w = call(k_sum, shape((16, 128)), (weights,))
    w = w + turn(w, 1) + turn(w, 2) + turn(w, 3)
    w_far = swap(w)
    g5, g7, g6 = turn(g4, 3), turn(g4, 1), turn(g4, 2)
    local, hubs = call(
        k_back, [block, shape((32, 8, 128))],
        (flag, *lists, grad_sum, g1, g2, g3, g4, g5, g6, g7, bwd), [sm, *lm] + [vm] * 9,
        [pltpu.VMEM((512, 128), F32)],
    )
    factor = (256 * lax.axis_size("grp") * lax.axis_size("blk")) ** (-0.5)
    last, grad_bias = call(
        functools.partial(k_pack, factor), [shape((32, 16, 128)), shape((1, 128))], (hubs, w, w_far)
    )
    last = exchange(last, "grp")
    local = call(k_scatter, block, (returned, send, local, grad_pre, w_root))
    grad_features, grad_wn, grad_wr = call(
        k_final, [block, shape((128, 128)), shape((128, 128))], (last, hub, local), [vm, sm, vm]
    )
    return output, grad_features, grad_wn, grad_wr, grad_bias.reshape(128)


def solution(mesh):
    rows = P(("grp", "blk"), None)
    in_specs = (
        rows, P(), P(), P(), rows,
        P("grp", "blk", None, None, None),
        P("grp", "blk", None, None, None, None),
        P("grp", "blk", None, None),
        P("grp", "blk", None), P("grp", "blk", None), P("grp", "blk", None), P("grp", "blk", None), P("grp", "blk", None),
    )
    return jax.shard_map(
        per_device, mesh=mesh, in_specs=in_specs, out_specs=(rows, rows, P(), P(), P()), check_vma=False
    )
```
